256 devices in a mesh: role: 2 (over core), expert: 8 (over z), shard: 16 (over x, y).
Axes of the slice: x: 4, y: 4, z: 8, core: 2. Of those that a mesh axis runs over, the one named last changes fastest.
Arguments:
- query: bfloat16 [512, 6144], P(('expert', 'shard'), 'role')
- new_kv: bfloat16 [512, 2, 1024], P(('expert', 'shard'), None, 'role'), may hold values from -6 to 6
- kv_cache: bfloat16 [512, 2, 128, 1024], P(('expert', 'shard'), None, None, 'role')
- lengths: int32 [512], P(('expert', 'shard')), may hold values from 32 to 128
- residual: bfloat16 [512, 6144], P(('expert', 'shard'), 'role'), may hold values from -8 to 8
- norm_gain: bfloat16 [6144], P('role'), may hold values from 0.099609375 to 1.8984375
- expert_ids: int32 [512, 2], P(('expert', 'shard')), may hold values from 0 to 7, all different within a row; in each aligned block of 4 rows (0 to 3, 4 to 7, ...) at most 2 rows name the same one
- router_logits: float32 [512, 8], P(('expert', 'shard')), may hold values from -0.75 to 0.75
- w_gate: bfloat16 [8, 6144, 8192], P('expert', 'role', 'shard'), may hold values from -0.078125 to 0.078125
- w_up: bfloat16 [8, 6144, 8192], P('expert', 'role', 'shard'), may hold values from -0.078125 to 0.078125
- w_down: bfloat16 [8, 8192, 6144], P('expert', 'shard', 'role'), may hold values from -0.0625 to 0.0625
Outputs:
- layer_out: bfloat16 [512, 6144], P(('expert', 'shard'), 'role')
The draws below stay inside these ranges and needn't reach their ends.
Inputs may be any that keep to these rules, and one draw needn't show every extreme that they name: `expert_ids`: the requests of one device name each expert at most 2 times.
All inputs are finite; a program needn't handle non-finite values.
Results may differ from the reference program's by a relative error of at most 0.0065.
Values may be sent and summed in bfloat16 or wider, within the bound.
No kernel may reach another device: no remote copies, remote signals or barrier semaphores. Data moves between devices by JAX's collectives and lax.ppermute only.
A program may use at most 64 MiB of HBM per device.

```python
import math
import jax
import jax.numpy as jnp
import numpy as np
from jax import lax

MODEL_WIDTH = 6144
HEADS = 48
KV_HEADS = 8
HD = 128
FF = 8192
REQ_DEV = 4
CTX = 128
TOP = 2
EXPERT_CAPACITY = 2
EXPERTS = 8
REQUESTS = 512


def leading_keys(key):
    return jax.random.normal(jax.random.fold_in(key, 101), (REQUESTS, 2, KV_HEADS * HD), jnp.float32)


def draw_kv_cache(key, part):
    lead = leading_keys(key)
    key = jax.random.fold_in(key, 7)
    base = jax.random.normal(key, (REQUESTS, 2, CTX, KV_HEADS * HD), jnp.float32)
    first = lead[:, 0]
    second = lead[:, 1]
    base = base.at[:, 0, 0].set(first).at[:, 0, 1].set(second)
    return base.astype(jnp.bfloat16)


def draw_query(key, part):
    key = jax.random.fold_in(key, 11)
    values = jax.random.normal(key, (REQUESTS, HEADS * HD), jnp.float32)
    return values.astype(jnp.bfloat16)


def feature_scales(low, high):
    position = jnp.arange(MODEL_WIDTH, dtype=jnp.float32) / (MODEL_WIDTH - 1)
    return jnp.exp(jnp.log(low) + position * (jnp.log(high) - jnp.log(low)))


def draw_residual(key, part):
    key = jax.random.fold_in(key, 23)
    values = jnp.clip(jax.random.normal(key, (REQUESTS, MODEL_WIDTH), jnp.float32), -4.0, 4.0)
    values = values * feature_scales(0.5, 2.0)[None, :]
    return values.astype(jnp.bfloat16)


def set_ends(array, key, smallest, high):
    shape = array.shape
    place = [jax.random.randint(jax.random.fold_in(key, axis), (), 0, shape[axis]) for axis in range(len(shape))]
    array = array.at[tuple(place)].set(smallest)
    longest = shape.index(max(shape))
    place[longest] = (place[longest] + 1) % shape[longest]
    return array.at[tuple(place)].set(high)


def block_scale(rng, dims, cuts, low, largest):
    level = 1.0
    for axis_at, parts in cuts:
        heights = jax.random.uniform(jax.random.fold_in(jax.random.fold_in(rng, 6), axis_at), (parts,), jnp.float32, low / len(cuts), largest / len(cuts))
        level = level * jnp.repeat(jnp.exp(heights), dims[axis_at] // parts).reshape((-1,) + (1,) * (len(dims) - 1 - axis_at))
    return level


def shared_out(own_key, own, number, rows, count, top, limit, slope):
    ranking = jax.random.permutation(own_key, count)
    packed, ordinary = shares(count, rows * top, limit, slope, True), shares(count, rows * top, limit, slope, False)
    places = jnp.arange(count)

    def named(tallies, rotation):
        used = int((tallies > 0).sum())
        fixed = max(1, used // 4)
        shifted = fixed + (places - fixed + rotation * (used - fixed)) % max(1, count - fixed)
        return jnp.zeros((count,), jnp.int32).at[ranking[jnp.where(places < fixed, places, shifted)]].set(jnp.asarray(tallies, jnp.int32))

    tallies = jnp.where(number % 4 == 0, named(packed, number // 4), named(ordinary, number - number // 4 - 1))
    mixed = jax.random.permutation(jax.random.fold_in(own, 3), count)
    donor, taker = mixed[0:count // 2 * 2:2], mixed[1:count // 2 * 2:2]
    margin = jnp.minimum(tallies[donor] - 1, limit - tallies[taker]) // 2
    margin = jnp.where((donor == ranking[0]) | (taker == ranking[0]) | (tallies[taker] == 0), 0, jnp.maximum(margin, 0))
    shifted = jax.random.randint(jax.random.fold_in(own, 4), (count // 2,), 0, 1 << 20) % (margin + 1)
    tallies = tallies.at[donor].add(-shifted).at[taker].add(shifted)
    members = jnp.searchsorted(jnp.cumsum(tallies), jnp.arange(rows * top), side="right").astype(jnp.int32)
    table = members.reshape(top, rows).T
    table = table[jax.random.permutation(jax.random.fold_in(own, 1), rows)]
    rotation = jax.random.randint(jax.random.fold_in(own, 2), (rows, 1), 0, top)
    return jnp.take_along_axis(table, (jnp.arange(top)[None, :] + rotation) % top, axis=1)


def shares(number_of, total, most, skew, full):
    loads = [(1 << 20) // math.isqrt(grade ** skew) + 1 for grade in range(1, number_of + 1)]
    largest = most if full else min(most, max(-(-total // number_of), total * loads[0] // sum(loads)))
    least = 1 if total - largest >= number_of - 1 else 0
    holding, spare = [largest] + [least] * (number_of - 1), total - largest - least * (number_of - 1)
    while spare > 0:
        free = [i for i in range(1, number_of) if holding[i] < largest] or [i for i in range(1, number_of) if holding[i] < most]
        mass, budget = sum([loads[i] for i in free]), spare
        for i in free:
            more = min(most - holding[i], max(1, budget * loads[i] // mass), spare)
            holding[i] = holding[i] + more
            spare = spare - more
    return np.array(holding)


def normal_values(stream_key, dims, width, most, shards=(), held_as=jnp.bfloat16):
    values = width * jax.random.normal(stream_key, dims, jnp.float32)
    if shards:
        values = values * block_scale(stream_key, dims, shards, -0.22, 0.18)
    return jnp.clip(values, -most, most).astype(held_as)


def setup_inputs(seed: int = 0) -> dict:
    key_of = jax.random.split(jax.random.key(seed), 12)
    query = draw_query(jax.random.fold_in(key_of[11], 71), 0)
    new_kv = normal_values(key_of[1], (REQUESTS, 2, KV_HEADS * HD), 1.0, 6.0, ((0, 128), (2, 2)))
    kv_cache = draw_kv_cache(jax.random.fold_in(key_of[11], 71), 0)
    lengths = set_ends(jax.random.randint(key_of[3], (REQUESTS,), CTX // 4, CTX + 1), jax.random.fold_in(key_of[3], 1), CTX // 4, CTX).astype(jnp.int32)
    residual = draw_residual(jax.random.fold_in(key_of[11], 71), 0)
    norm_gain = jnp.clip(1.0 + 0.18 * jax.random.normal(key_of[5], (MODEL_WIDTH,), jnp.float32), 0.099609375, 1.8984375).astype(jnp.bfloat16)
    expert_ids_keys = jax.random.split(jax.random.fold_in(key_of[6], 1), REQUESTS // REQ_DEV)
    expert_ids_turns = jax.random.permutation(jax.random.fold_in(key_of[6], 3), REQUESTS // REQ_DEV)
    expert_ids = jax.vmap(lambda own, number: shared_out(jax.random.fold_in(key_of[6], 2), own, number, REQ_DEV, EXPERTS, TOP, EXPERT_CAPACITY, 2))(expert_ids_keys, expert_ids_turns).reshape((REQUESTS, TOP))
    router_logits = jnp.clip(jax.random.uniform(key_of[7], (REQUESTS, EXPERTS), jnp.float32, -0.75, 0.75) * block_scale(key_of[7], (REQUESTS, EXPERTS), ((0, 128),), -0.4, 0.0), -0.75, 0.75)
    w_gate = normal_values(key_of[8], (EXPERTS, MODEL_WIDTH, FF), MODEL_WIDTH ** -0.5, 0.078125, ((0, 8), (1, 2), (2, 16)))
    w_up = normal_values(key_of[9], (EXPERTS, MODEL_WIDTH, FF), MODEL_WIDTH ** -0.5, 0.078125, ((0, 8), (1, 2), (2, 16)))
    w_down = normal_values(key_of[10], (EXPERTS, FF, MODEL_WIDTH), FF ** -0.5, 0.0625, ((0, 8), (1, 16), (2, 2)))
    return {"query": query, "new_kv": new_kv, "kv_cache": kv_cache, "lengths": lengths, "residual": residual, "norm_gain": norm_gain, "expert_ids": expert_ids, "router_logits": router_logits, "w_gate": w_gate, "w_up": w_up, "w_down": w_down}


def reference(query, new_kv, kv_cache, lengths, residual, norm_gain, expert_ids, router_logits, w_gate, w_up, w_down):
    group = HEADS // KV_HEADS
    scale = 1.0 / HD ** 0.5
    q = query.astype(jnp.float32).reshape(REQUESTS, KV_HEADS, group, HD)
    keys = kv_cache[:, 0].astype(jnp.float32).reshape(REQUESTS, CTX, KV_HEADS, HD)
    values = kv_cache[:, 1].astype(jnp.float32).reshape(REQUESTS, CTX, KV_HEADS, HD)
    new_k = new_kv[:, 0].astype(jnp.float32).reshape(REQUESTS, KV_HEADS, HD)
    new_v = new_kv[:, 1].astype(jnp.float32).reshape(REQUESTS, KV_HEADS, HD)
    scores = jnp.einsum('rkgd,rckd->rkgc', q, keys) * scale
    own = jnp.einsum('rkgd,rkd->rkg', q, new_k) * scale
    valid = (jnp.arange(CTX, dtype=jnp.int32)[None, :] < lengths[:, None])[:, None, None, :]
    top = jnp.maximum(lax.optimization_barrier(jnp.max(jnp.where(valid, scores, -jnp.inf), axis=-1)), own)
    ecache = jnp.where(valid, jnp.exp(scores - top[..., None]), 0.0)
    eown = jnp.exp(own - top)
    total = lax.optimization_barrier(jnp.sum(ecache, axis=-1)) + eown
    pcache = (ecache / total[..., None]).astype(jnp.bfloat16).astype(jnp.float32)
    pown = (eown / total).astype(jnp.bfloat16).astype(jnp.float32)
    attn = jnp.einsum('rkgc,rckd->rkgd', pcache, values) + pown[..., None] * new_v[:, :, None, :]
    hidden = (residual.astype(jnp.float32) + attn.reshape(REQUESTS, MODEL_WIDTH)).astype(jnp.bfloat16)
    hf = hidden.astype(jnp.float32)
    meansq = lax.optimization_barrier(jnp.mean(hf * hf, axis=-1, keepdims=True))
    normed = (hf * lax.rsqrt(meansq + 1e-05) * norm_gain.astype(jnp.float32)).astype(jnp.bfloat16)
    block_list = REQUESTS // REQ_DEV
    pairs = REQ_DEV * TOP
    flat = expert_ids.reshape(block_list, pairs)
    onehot = (flat[..., None] == jnp.arange(EXPERTS, dtype=jnp.int32)).astype(jnp.int32)
    rank = jnp.cumsum(onehot, axis=1) - onehot
    slot = lax.optimization_barrier(jnp.sum(rank * onehot, axis=-1))
    slot_hit = (slot[..., None] == jnp.arange(EXPERT_CAPACITY, dtype=jnp.int32)).astype(jnp.float32)
    select = jnp.einsum('bpe,bpc->becp', onehot.astype(jnp.float32), slot_hit)
    owner = (jnp.arange(pairs, dtype=jnp.int32)[:, None] // TOP == jnp.arange(REQ_DEV, dtype=jnp.int32)[None, :]).astype(jnp.float32)
    logits = router_logits.reshape(block_list, REQ_DEV, EXPERTS)
    chosen = jnp.einsum('brte,bre->brt', onehot.astype(jnp.float32).reshape(block_list, REQ_DEV, TOP, EXPERTS), logits, precision=lax.Precision.HIGHEST)
    weights = jnp.stack([jax.nn.sigmoid(chosen[..., 0] - chosen[..., 1]), jax.nn.sigmoid(chosen[..., 1] - chosen[..., 0])], axis=-1).reshape(block_list, pairs)
    feature_count = normed.astype(jnp.float32).reshape(block_list, REQ_DEV, MODEL_WIDTH)
    moe = jnp.zeros((block_list, pairs, MODEL_WIDTH), jnp.float32)
    for e in range(EXPERTS):
        dispatch_rows = jnp.einsum('bcp,pq->bcq', select[:, e], owner)
        token_rows = jnp.einsum('veu,vuh->veh', dispatch_rows, feature_count, precision=lax.Precision.HIGHEST).astype(jnp.bfloat16).reshape(block_list * EXPERT_CAPACITY, MODEL_WIDTH)
        gate = jnp.dot(token_rows, w_gate[e], preferred_element_type=jnp.float32)
        up = jnp.dot(token_rows, w_up[e], preferred_element_type=jnp.float32)
        act = (jax.nn.silu(gate) * up).astype(jnp.bfloat16)
        out = jnp.dot(act, w_down[e], preferred_element_type=jnp.float32).astype(jnp.bfloat16)
        out = out.astype(jnp.float32).reshape(block_list, EXPERT_CAPACITY, MODEL_WIDTH)
        moe = moe + jnp.einsum('bcp,bcd->bpd', select[:, e] * weights[:, None, :], out, precision=lax.Precision.HIGHEST)
    moe = lax.optimization_barrier(jnp.sum(moe.reshape(block_list, REQ_DEV, TOP, MODEL_WIDTH), axis=2)).reshape(REQUESTS, MODEL_WIDTH)
    return (hf + moe).astype(jnp.bfloat16)
```

```python
import functools

import jax
import jax.numpy as jnp
from jax import lax
from jax.experimental import pallas as pl
from jax.experimental.pallas import tpu as pltpu
from jax.sharding import Mesh
from jax.sharding import PartitionSpec as P

MODEL_WIDTH = 6144
HALF = 3072
GROUP = 6
HD = 128
CTX = 128
ROWS = 4
LOCAL_HEADS = 4
EXPERTS = 8
CAP = 2
HIDDEN = 512
AXES = ("role", "expert", "x", "y")
SHIFTS = (0, 1, -1, 2)
VMEM_SPEC = pl.BlockSpec(memory_space=pltpu.VMEM)
SMEM_SPEC = pl.BlockSpec(memory_space=pltpu.SMEM)
F32 = jnp.float32
BF16 = jnp.bfloat16


def call(body, out_shape, in_specs, flops=0, nbytes=0, scratch=()):
    single = not isinstance(out_shape, (tuple, list))
    out_specs = VMEM_SPEC if single else [VMEM_SPEC] * len(out_shape)
    return pl.pallas_call(
        body,
        out_shape=out_shape,
        in_specs=in_specs,
        out_specs=out_specs,
        scratch_shapes=list(scratch),
        compiler_params=pltpu.CompilerParams(vmem_limit_bytes=40 * 1024 * 1024),
        cost_estimate=pl.CostEstimate(flops=flops, bytes_accessed=nbytes, transcendentals=0),
    )


def attend_body(len_ref, q_ref, new_ref, kv_ref, res_ref, hidden_ref, sq_ref):
    scale = 1.0 / HD**0.5
    m_rows = GROUP * ROWS
    row_req = lax.broadcasted_iota(jnp.int32, (m_rows, 1), 0) % ROWS
    row_len = jnp.zeros((m_rows, 1), jnp.int32)
    for r in range(ROWS):
        row_len = jnp.where(row_req == r, len_ref[r], row_len)
    col = lax.broadcasted_iota(jnp.int32, (m_rows, ROWS * CTX), 1)
    valid = (col // CTX == row_req) & (col % CTX < row_len)
    own_valid = lax.broadcasted_iota(jnp.int32, (m_rows, ROWS), 1) == row_req
    nt = (((1,), (1,)), ((), ()))
    acc = jnp.zeros((ROWS, HD), F32)
    new = new_ref[...].astype(F32)
    for k in range(LOCAL_HEADS):
        sl = slice(k * HD, (k + 1) * HD)
        q = jnp.concatenate(
            [
                q_ref[:, (k * GROUP + g) * HD : (k * GROUP + g + 1) * HD].astype(F32)
                for g in range(GROUP)
            ],
            axis=0,
        ).astype(BF16)
        keys = kv_ref[:, 0, :, sl].reshape(ROWS * CTX, HD)
        vals = kv_ref[:, 1, :, sl].reshape(ROWS * CTX, HD)
        nk = new[:, 0, sl].astype(BF16)
        nv = new[:, 1, sl].astype(BF16)
        s = lax.dot_general(q, keys, nt, preferred_element_type=F32) * scale
        so = lax.dot_general(q, nk, nt, preferred_element_type=F32) * scale
        s = jnp.where(valid, s, -jnp.inf)
        so = jnp.where(own_valid, so, -jnp.inf)
        top = jnp.maximum(
            jnp.max(s, axis=1, keepdims=True), jnp.max(so, axis=1, keepdims=True)
        )
        e = jnp.exp(s - top)
        eo = jnp.exp(so - top)
        total = jnp.sum(e, axis=1, keepdims=True) + jnp.sum(eo, axis=1, keepdims=True)
        p = (e / total).astype(BF16)
        po = (eo / total).astype(BF16)
        attn = jnp.dot(p, vals, preferred_element_type=F32) + jnp.dot(
            po, nv, preferred_element_type=F32
        )
        for g in range(GROUP):
            h = k * GROUP + g
            hs = slice(h * HD, (h + 1) * HD)
            hid = (res_ref[:, hs].astype(F32) + attn[g * ROWS : (g + 1) * ROWS]).astype(BF16)
            hidden_ref[:, hs] = hid
            hf = hid.astype(F32)
            acc = acc + hf * hf
    sq_ref[...] = acc


def slot_rows(ids):
    rows = []
    for p in range(len(ids)):
        slot = jnp.int32(0)
        for q in range(p):
            slot = slot + (ids[q] == ids[p]).astype(jnp.int32)
        rows.append(ids[p] * CAP + slot)
    return rows


def dispatch_body(ids_ref, hidden_ref, sq_ref, sq2_ref, gain_ref, out_ref):
    ids = [ids_ref[p // 2, p % 2] for p in range(2 * ROWS)]
    rows = slot_rows(ids)
    total = jnp.sum(sq_ref[...] + sq2_ref[...], axis=1, keepdims=True)
    inv = lax.rsqrt(total / MODEL_WIDTH + 1e-05)
    normed = (hidden_ref[...].astype(F32) * inv * gain_ref[...].astype(F32)).astype(BF16)
    ri = lax.broadcasted_iota(jnp.int32, (EXPERTS * CAP, ROWS), 0)
    ci = lax.broadcasted_iota(jnp.int32, (EXPERTS * CAP, ROWS), 1)
    select = jnp.zeros((EXPERTS * CAP, ROWS), F32)
    for p in range(2 * ROWS):
        select = jnp.where((ri == rows[p]) & (ci == p // 2), 1.0, select)
    out = jnp.dot(select.astype(BF16), normed, preferred_element_type=F32).astype(BF16)
    for e in range(EXPERTS):
        out_ref[e] = out[e * CAP : (e + 1) * CAP]


def gate_body(x0, x1, x2, x3, wg_ref, wu_ref, own_ref, send_ref):
    x = jnp.concatenate([x0[...], x1[...], x2[...], x3[...]], axis=0)
    for n in range(0, HIDDEN, 256):
        for at, w_ref in ((0, wg_ref), (HIDDEN, wu_ref)):
            got = jnp.dot(x, w_ref[:, n : n + 256], preferred_element_type=F32)
            own_ref[:, at + n : at + n + 256] = got
            send_ref[:, at + n : at + n + 256] = got.astype(BF16)


def down_body(own_ref, got_ref, wd_ref, o0, o1, o2, o3, act_ref):
    for jb in range(4):
        for ja in range(4):
            at = (jb * 4 + ja) * 16
            peer = (ja * 4 + jb) * 16
            pre = own_ref[at : at + 16] + got_ref[peer : peer + 16].astype(F32)
            gate = pre[:, :HIDDEN]
            act_ref[at : at + 16] = (gate * jax.nn.sigmoid(gate) * pre[:, HIDDEN:]).astype(BF16)
    outs = (o0, o1, o2, o3)
    act = act_ref[...]
    for n in range(0, HALF, 512):
        got = jnp.dot(act, wd_ref[:, n : n + 512], preferred_element_type=F32).astype(BF16)
        for j in range(4):
            outs[j][:, n : n + 512] = got[j * 64 : (j + 1) * 64]


def combine_body(ids_ref, logit_ref, hidden_ref, back_ref, out_ref):
    ids = [ids_ref[p // 2, p % 2] for p in range(2 * ROWS)]
    rows = slot_rows(ids)
    ci = lax.broadcasted_iota(jnp.int32, (CAP, 1), 0)
    for t in range(ROWS):
        a, b = ids[2 * t], ids[2 * t + 1]
        diff = jnp.full((CAP, 1), logit_ref[t, a] - logit_ref[t, b], F32)
        wa = jnp.where(ci == rows[2 * t] - a * CAP, jax.nn.sigmoid(diff), 0.0)
        wb = jnp.where(ci == rows[2 * t + 1] - b * CAP, jax.nn.sigmoid(-diff), 0.0)
        both = back_ref[a].astype(F32) * wa + back_ref[b].astype(F32) * wb
        moe = jnp.sum(both, axis=0, keepdims=True)
        out_ref[t : t + 1] = (hidden_ref[t : t + 1].astype(F32) + moe).astype(BF16)


def index_of(role, z, x, y):
    return ((role * 8 + z) * 4 + x) * 4 + y


def permutation(move):
    return [
        (index_of(r, z, x, y), index_of(*move(r, z, x, y)))
        for r in range(2)
        for z in range(8)
        for x in range(4)
        for y in range(4)
    ]


def along_x(s, r, z, x, y):
    return r, z, (x + s) % 4, y


def along_y(s, r, z, x, y):
    return r, z, x, (y + s) % 4


def ring(which, s):
    def move(r, z, x, y):
        first = along_x if (r == 0) == (which == 0) else along_y
        return first(s, r, z, x, y)

    return permutation(move)


def send(value, which, s):
    return lax.ppermute(value, AXES, ring(which, s))


def swap(value):
    return lax.ppermute(value, "role", [(0, 1), (1, 0)])


def add_up(parts):
    total = parts[0].astype(F32)
    for p in parts[1:]:
        total = total + p.astype(F32)
    return total.astype(BF16)


def per_device(
    query, new_kv, kv_cache, lengths, residual, norm_gain, expert_ids, router_logits, w_gate, w_up, w_down
):
    hidden, sq = call(
        attend_body,
        (jax.ShapeDtypeStruct((ROWS, HALF), BF16), jax.ShapeDtypeStruct((ROWS, HD), F32)),
        [SMEM_SPEC] + [VMEM_SPEC] * 4,
        flops=50_000_000,
        nbytes=1_200_000,
    )(lengths, query, new_kv, kv_cache, residual)
    outgoing = call(
        dispatch_body,
        jax.ShapeDtypeStruct((EXPERTS, CAP, HALF), BF16),
        [SMEM_SPEC] + [VMEM_SPEC] * 4,
        flops=400_000,
        nbytes=150_000,
    )(expert_ids, hidden, sq, swap(sq), norm_gain.reshape(1, HALF))
    arrived = lax.all_to_all(outgoing, "expert", split_axis=0, concat_axis=0, tiled=True)
    block = arrived.reshape(EXPERTS * CAP, HALF)
    plane = jnp.concatenate([block] + [send(block, 0, s) for s in SHIFTS[1:]], axis=0)
    pieces = [plane] + [send(plane, 1, s) for s in SHIFTS[1:]]
    own, partial = call(
        gate_body,
        (jax.ShapeDtypeStruct((256, 2 * HIDDEN), F32), jax.ShapeDtypeStruct((256, 2 * HIDDEN), BF16)),
        [VMEM_SPEC] * 6,
        flops=2 * 256 * HALF * 1024,
        nbytes=9_000_000,
    )(*pieces, w_gate[0], w_up[0])
    terms = call(
        down_body,
        [jax.ShapeDtypeStruct((64, HALF), BF16)] * 4,
        [VMEM_SPEC] * 3,
        flops=2 * 256 * HALF * 512,
        nbytes=6_000_000,
        scratch=[pltpu.VMEM((256, HIDDEN), BF16)],
    )(own, swap(partial), w_down[0])
    rows_b = add_up([terms[0]] + [send(terms[j], 1, -SHIFTS[j]) for j in (1, 2, 3)])
    parts = [rows_b[16 * j : 16 * j + 16] for j in range(4)]
    rows_a = add_up([parts[0]] + [send(parts[j], 0, -SHIFTS[j]) for j in (1, 2, 3)])
    back = lax.all_to_all(
        rows_a.reshape(EXPERTS, CAP, HALF), "expert", split_axis=0, concat_axis=0, tiled=True
    )
    return call(
        combine_body,
        jax.ShapeDtypeStruct((ROWS, HALF), BF16),
        [SMEM_SPEC] * 2 + [VMEM_SPEC] * 2,
        flops=100_000,
        nbytes=150_000,
    )(expert_ids, router_logits, hidden, back)


def solution(mesh):
    fine = Mesh(mesh.devices.reshape(2, 8, 4, 4), AXES)
    rows = ("expert", "x", "y")
    shard = ("x", "y")
    in_specs = (
        P(rows, "role"),
        P(rows, None, "role"),
        P(rows, None, None, "role"),
        P(rows),
        P(rows, "role"),
        P("role"),
        P(rows, None),
        P(rows, None),
        P("expert", "role", shard),
        P("expert", "role", shard),
        P("expert", shard, "role"),
    )
    return jax.shard_map(
        per_device, mesh=fine, in_specs=in_specs, out_specs=P(rows, "role"), check_vma=False
    )
```

```python
import jax
import jax.numpy as jnp
from jax import lax
from jax.experimental import pallas as pl
from jax.experimental.pallas import tpu as pltpu
from jax.sharding import Mesh
from jax.sharding import PartitionSpec as P

MODEL_WIDTH = 6144
HALF = 3072
GROUP = 6
HD = 128
CTX = 128
ROWS = 4
LOCAL_HEADS = 4
EXPERTS = 8
CAP = 2
HIDDEN = 512
AXES = ("role", "expert", "x", "y")
SHIFTS = (0, 1, -1, 2)
VMEM_SPEC = pl.BlockSpec(memory_space=pltpu.VMEM)
HBM_SPEC = pl.BlockSpec(memory_space=pltpu.HBM)
F32 = jnp.float32
BF16 = jnp.bfloat16


def call(body, out_shape, in_specs, flops=0, nbytes=0, scratch=()):
    single = not isinstance(out_shape, (tuple, list))
    out_specs = VMEM_SPEC if single else [VMEM_SPEC] * len(out_shape)
    return pl.pallas_call(
        body,
        out_shape=out_shape,
        in_specs=in_specs,
        out_specs=out_specs,
        scratch_shapes=list(scratch),
        compiler_params=pltpu.CompilerParams(vmem_limit_bytes=16 * 1024 * 1024),
        cost_estimate=pl.CostEstimate(flops=flops, bytes_accessed=nbytes, transcendentals=0),
    )


def in_hbm(value):
    return pltpu.with_memory_space_constraint(value, pltpu.HBM)


def attend_body(
    len_hbm, ids_hbm, logit_hbm, q_hbm, new_hbm, kv_hbm, res_hbm,
    hidden_ref, out_ref, comb_ref,
    len_ref, ids_ref, logit_ref, q_ref, new_ref, k_ref, v_ref, res_ref, sems,
):
    pairs = (
        (kv_hbm.at[:, 0], k_ref),
        (q_hbm, q_ref),
        (len_hbm, len_ref),
        (new_hbm, new_ref),
        (kv_hbm.at[:, 1], v_ref),
        (res_hbm, res_ref),
        (ids_hbm, ids_ref),
        (logit_hbm, logit_ref),
    )
    copies = [pltpu.make_async_copy(a, b, sems.at[i]) for i, (a, b) in enumerate(pairs)]
    for c in copies:
        c.start()
    scale = 1.0 / HD**0.5
    m_rows = GROUP * ROWS
    nt = (((1,), (1,)), ((), ()))
    for c in copies[:4]:
        c.wait()
    row_req = lax.broadcasted_iota(jnp.int32, (m_rows, 1), 0) % ROWS
    row_len = jnp.zeros((m_rows, 1), jnp.int32)
    for r in range(ROWS):
        row_len = jnp.where(row_req == r, len_ref[r], row_len)
    col = lax.broadcasted_iota(jnp.int32, (m_rows, ROWS * CTX), 1)
    valid = (col // CTX == row_req) & (col % CTX < row_len)
    own_valid = lax.broadcasted_iota(jnp.int32, (m_rows, ROWS), 1) == row_req
    new = new_ref[...].astype(F32)
    scores, owns = [], []
    for k in range(LOCAL_HEADS):
        sl = slice(k * HD, (k + 1) * HD)
        q = jnp.concatenate(
            [
                q_ref[:, (k * GROUP + g) * HD : (k * GROUP + g + 1) * HD].astype(F32)
                for g in range(GROUP)
            ],
            axis=0,
        ).astype(BF16)
        keys = k_ref[:, :, sl].reshape(ROWS * CTX, HD)
        nk = new[:, 0, sl].astype(BF16)
        s = lax.dot_general(q, keys, nt, preferred_element_type=F32) * scale
        so = lax.dot_general(q, nk, nt, preferred_element_type=F32) * scale
        scores.append(jnp.where(valid, s, -jnp.inf))
        owns.append(jnp.where(own_valid, so, -jnp.inf))
    tops = [
        jnp.maximum(jnp.max(s, axis=1, keepdims=True), jnp.max(so, axis=1, keepdims=True))
        for s, so in zip(scores, owns)
    ]
    es = [jnp.exp(s - t) for s, t in zip(scores, tops)]
    eos = [jnp.exp(so - t) for so, t in zip(owns, tops)]
    totals = [
        jnp.sum(e, axis=1, keepdims=True) + jnp.sum(eo, axis=1, keepdims=True)
        for e, eo in zip(es, eos)
    ]
    for c in copies[4:]:
        c.wait()
    for k in range(LOCAL_HEADS):
        sl = slice(k * HD, (k + 1) * HD)
        vals = v_ref[:, :, sl].reshape(ROWS * CTX, HD)
        nv = new[:, 1, sl].astype(BF16)
        p = (es[k] / totals[k]).astype(BF16)
        po = (eos[k] / totals[k]).astype(BF16)
        attn = jnp.dot(p, vals, preferred_element_type=F32) + jnp.dot(
            po, nv, preferred_element_type=F32
        )
        for g in range(GROUP):
            h = k * GROUP + g
            hs = slice(h * HD, (h + 1) * HD)
            hidden_ref[:, hs] = (
                res_ref[:, hs].astype(F32) + attn[g * ROWS : (g + 1) * ROWS]
            ).astype(BF16)
    ids = [ids_ref[p % 2, p // 2] for p in range(2 * ROWS)]
    rows = slot_rows(ids)
    ri = lax.broadcasted_iota(jnp.int32, (EXPERTS * CAP, ROWS), 0)
    ci = lax.broadcasted_iota(jnp.int32, (EXPERTS * CAP, ROWS), 1)
    select = jnp.zeros((EXPERTS * CAP, ROWS), F32)
    for p in range(2 * ROWS):
        select = jnp.where((ri == rows[p]) & (ci == p // 2), 1.0, select)
    out = jnp.dot(select.astype(BF16), hidden_ref[...], preferred_element_type=F32).astype(BF16)
    for e in range(EXPERTS):
        for a in range(4):
            out_ref[a * EXPERTS + e] = out[e * CAP : (e + 1) * CAP]
    lane = lax.broadcasted_iota(jnp.int32, (ROWS, HD), 1)
    tok = lax.broadcasted_iota(jnp.int32, (ROWS, HD), 0)
    diff = jnp.zeros((ROWS, HD), F32)
    for t in range(ROWS):
        gap = logit_ref[t, ids[2 * t]] - logit_ref[t, ids[2 * t + 1]]
        diff = jnp.where(tok == t, gap, diff)
    wa, wb = jax.nn.sigmoid(diff), jax.nn.sigmoid(-diff)
    place = lane % (EXPERTS * CAP)
    comb = jnp.zeros((ROWS, HD), F32)
    for t in range(ROWS):
        comb = jnp.where((tok == t) & (place == rows[2 * t]), wa, comb)
        comb = jnp.where((tok == t) & (place == rows[2 * t + 1]), wb, comb)
    high = comb.astype(BF16).astype(F32)
    mid = (comb - high).astype(BF16).astype(F32)
    low = comb - high - mid
    comb_ref[...] = jnp.concatenate([high, mid, low, jnp.zeros_like(low)], axis=0).astype(BF16)


def slot_rows(ids):
    rows = []
    for p in range(len(ids)):
        slot = jnp.int32(0)
        for q in range(p):
            slot = slot + (ids[q] == ids[p]).astype(jnp.int32)
        rows.append(ids[p] * CAP + slot)
    return rows


CHUNK = 512


def weights_body(after_ref, gain_ref, wg_hbm, wu_hbm, wd_hbm, wg_ref, wu_ref, wd_ref, stage, sems):
    del after_ref
    steps = [(i, w) for i in range(HALF // CHUNK) for w in (0, 1)]
    sources, targets = (wg_hbm, wu_hbm), (wg_ref, wu_ref)

    def fetch(n):
        i, w = steps[n]
        return pltpu.make_async_copy(
            sources[w].at[0, pl.ds(i * CHUNK, CHUNK)], stage.at[n], sems.at[n]
        )

    down = pltpu.make_async_copy(wd_hbm.at[0], wd_ref, sems.at[len(steps)])
    for n in range(len(steps)):
        fetch(n).start()
    down.start()
    for n, (i, w) in enumerate(steps):
        fetch(n).wait()
        for r in range(CHUNK // HD):
            at = i * CHUNK + r * HD
            row = gain_ref[:, at : at + HD].astype(F32)
            tile = jnp.transpose(jnp.broadcast_to(row, (HD, HD)))
            for c in range(HIDDEN // HD):
                cs = slice(c * HD, (c + 1) * HD)
                part = stage[n, r * HD : (r + 1) * HD, cs].astype(F32) * tile
                targets[w][at : at + HD, cs] = part.astype(BF16)
    down.wait()


def gate_body(x0, x1, wg_ref, wu_ref, own_ref, sq_ref, send_ref):
    half = x0.shape[0]
    x = jnp.concatenate([x0[...], x1[...]], axis=0)
    for at, w_ref in ((0, wg_ref), (HIDDEN, wu_ref)):
        got = jnp.dot(x, w_ref[...], preferred_element_type=F32)
        own_ref[:, at : at + HIDDEN] = got
        send_ref[:, at : at + HIDDEN] = got.astype(BF16)
    lane = lax.broadcasted_iota(jnp.int32, (half, HD), 1)
    for n, x_ref in enumerate((x0, x1)):
        acc = jnp.zeros((half, HD), F32)
        for c in range(0, HALF, HD):
            part = x_ref[:, c : c + HD].astype(F32)
            acc = acc + part * part
        total = jnp.broadcast_to(jnp.sum(acc, axis=1, keepdims=True), (half, HD))
        high = total.astype(BF16).astype(F32)
        low = jnp.where(high < jnp.inf, total - high, 0.0)
        sq_ref[n * half : (n + 1) * half] = total
        send_ref[n * half : (n + 1) * half, 2 * HIDDEN :] = jnp.where(
            lane < HD // 2, high, low
        ).astype(BF16)


PLACES = {0: (0, 0), 3: (0, 64), 1: (1, 0), 2: (1, 64)}


def coordinates():
    role, x, y = (lax.axis_index(n) for n in ("role", "x", "y"))
    return jnp.where(role == 0, x, y), jnp.where(role == 0, y, x)


def block_at(start, place, shift):
    return pl.ds(pl.multiple_of(start + lax.rem(place - shift + 4, 4) * 16, 16), 16)


def down_body(own0, sq0, own1, sq1, got0, got1, wd_ref, o0, o1, o2, o3, act_ref):
    owns, sqs, gots = (own0, own1), (sq0, sq1), (got0, got1)
    my_a, my_b = coordinates()
    for jb in range(4):
        for ja in range(4):
            h, at = PLACES[jb]
            ph, pat = PLACES[ja]
            mine = block_at(at, my_a, SHIFTS[ja])
            peer = block_at(pat, my_b, SHIFTS[jb])
            got = gots[ph][peer].astype(F32)
            lane = 2 * HIDDEN
            extra = got[:, lane : lane + 1] + got[:, lane + HD // 2 : lane + HD // 2 + 1]
            total = sqs[h][mine][:, :1] + extra
            inv = lax.rsqrt(total / MODEL_WIDTH + 1e-05)
            pre = owns[h][mine] + got[:, : 2 * HIDDEN]
            pre = jnp.where(inv > 0.0, pre * inv, 0.0)
            gate = pre[:, :HIDDEN]
            place = (jb * 4 + ja) * 16
            act_ref[place : place + 16] = (gate * jax.nn.sigmoid(gate) * pre[:, HIDDEN:]).astype(BF16)
    outs = (o0, o1, o2, o3)
    act = act_ref[...]
    for n in range(0, HALF, 512):
        got = jnp.dot(act, wd_ref[:, n : n + 512], preferred_element_type=F32).astype(BF16)
        for j in range(4):
            outs[j][:, n : n + 512] = got[j * 64 : (j + 1) * 64]


def gather_body(t0, t1, t2, t3, out_ref):
    my_a, _ = coordinates()
    for ja in range(4):
        at = slice(16 * ja, 16 * ja + 16)
        total = t0[at].astype(F32) + t1[at].astype(F32) + t2[at].astype(F32) + t3[at].astype(F32)
        out_ref[block_at(0, my_a, SHIFTS[ja])] = total.astype(BF16)


def combine_body(comb_ref, hidden_ref, back_ref, out_ref):
    got = jnp.dot(comb_ref[:, :64], back_ref[...], preferred_element_type=F32)
    moe = got[:ROWS] + got[ROWS : 2 * ROWS] + got[2 * ROWS : 3 * ROWS]
    out_ref[...] = (hidden_ref[...].astype(F32) + moe).astype(BF16)


def index_of(role, z, x, y):
    return ((role * 8 + z) * 4 + x) * 4 + y


def permutation(move):
    return [
        (index_of(r, z, x, y), index_of(*move(r, z, x, y)))
        for r in range(2)
        for z in range(8)
        for x in range(4)
        for y in range(4)
    ]


def along_x(s, r, z, x, y):
    return r, z, (x + s) % 4, y


def along_y(s, r, z, x, y):
    return r, z, x, (y + s) % 4


def send(value, s):
    return lax.ppermute(
        value,
        AXES,
        permutation(lambda r, z, x, y: along_y(s, r, z, x, y) if r == 0 else along_x(s, r, z, x, y)),
    )


def swap(value):
    return lax.ppermute(value, "role", [(0, 1), (1, 0)])


def exchange(value):
    groups = [[index_of(0, z, x, y) for x in range(4) for z in range(8)] for y in range(4)]
    groups += [[index_of(1, z, x, y) for y in range(4) for z in range(8)] for x in range(4)]
    return lax.all_to_all(
        value, AXES, split_axis=0, concat_axis=0, axis_index_groups=groups, tiled=True
    )


def per_device(
    query, new_kv, kv_cache, lengths, residual, norm_gain, expert_ids, router_logits, w_gate, w_up, w_down
):
    shape = jax.ShapeDtypeStruct
    hidden, outgoing, comb = call(
        attend_body,
        (shape((ROWS, HALF), BF16), shape((4 * EXPERTS, CAP, HALF), BF16), shape((4 * ROWS, HD), BF16)),
        [HBM_SPEC] * 7,
        flops=50_000_000,
        nbytes=1_200_000,
        scratch=[
            pltpu.SMEM((ROWS,), jnp.int32),
            pltpu.SMEM((2, ROWS), jnp.int32),
            pltpu.SMEM((ROWS, EXPERTS), F32),
            pltpu.VMEM((ROWS, HALF), BF16),
            pltpu.VMEM((ROWS, 2, HIDDEN), BF16),
            pltpu.VMEM((ROWS, CTX, HIDDEN), BF16),
            pltpu.VMEM((ROWS, CTX, HIDDEN), BF16),
            pltpu.VMEM((ROWS, HALF), BF16),
            pltpu.SemaphoreType.DMA((8,)),
        ],
    )(*map(in_hbm, (lengths, expert_ids.T, router_logits, query, new_kv, kv_cache, residual)))
    plane = exchange(outgoing).reshape(64, HALF)
    count = 2 * HALF // CHUNK
    wg, wu, wd = call(
        weights_body,
        (
            pltpu.VMEM((HALF, HIDDEN), BF16),
            pltpu.VMEM((HALF, HIDDEN), BF16),
            pltpu.VMEM((HIDDEN, HALF), BF16),
        ),
        [HBM_SPEC, VMEM_SPEC, HBM_SPEC, HBM_SPEC, HBM_SPEC],
        flops=20_000_000,
        nbytes=18_000_000,
        scratch=[
            pltpu.VMEM((count, CHUNK, HIDDEN), BF16),
            pltpu.SemaphoreType.DMA((count + 1,)),
        ],
    )(plane, norm_gain.reshape(1, HALF), *map(in_hbm, (w_gate, w_up, w_down)))
    pieces = [plane] + [send(plane, s) for s in SHIFTS[1:]]

    def gate(x0, x1):
        return call(
            gate_body,
            (shape((128, 2 * HIDDEN), F32), shape((128, HD), F32), shape((128, 2 * HIDDEN + HD), BF16)),
            [VMEM_SPEC] * 4,
            flops=2 * 128 * HALF * 1024,
            nbytes=8_000_000,
        )(x0, x1, wg, wu)

    own0, sq0, send0 = gate(pieces[0], pieces[3])
    own1, sq1, send1 = gate(pieces[1], pieces[2])
    terms = call(
        down_body,
        [shape((64, HALF), BF16)] * 4,
        [VMEM_SPEC] * 7,
        flops=2 * 256 * HALF * 512,
        nbytes=6_000_000,
        scratch=[pltpu.VMEM((256, HIDDEN), BF16)],
    )(own0, sq0, own1, sq1, swap(send0), swap(send1), wd)
    summed = call(
        gather_body,
        shape((64, HALF), BF16),
        [VMEM_SPEC] * 4,
        flops=800_000,
        nbytes=2_000_000,
    )(terms[0], *[send(terms[j], -SHIFTS[j]) for j in (1, 2, 3)])
    back = exchange(summed.reshape(4 * EXPERTS, CAP, HALF)).reshape(64, HALF)
    return call(
        combine_body,
        shape((ROWS, HALF), BF16),
        [VMEM_SPEC] * 3,
        flops=100_000,
        nbytes=150_000,
    )(comb, hidden, back)


def solution(mesh):
    fine = Mesh(mesh.devices.reshape(2, 8, 4, 4), AXES)
    rows = ("expert", "x", "y")
    shard = ("x", "y")
    in_specs = (
        P(rows, "role"),
        P(rows, None, "role"),
        P(rows, None, None, "role"),
        P(rows),
        P(rows, "role"),
        P("role"),
        P(rows, None),
        P(rows, None),
        P("expert", "role", shard),
        P("expert", "role", shard),
        P("expert", shard, "role"),
    )
    return jax.shard_map(
        per_device, mesh=fine, in_specs=in_specs, out_specs=P(rows, "role"), check_vma=False
    )
```

```python
import jax
import jax.numpy as jnp
from jax import lax
from jax.experimental import pallas as pl
from jax.experimental.pallas import tpu as pltpu
from jax.sharding import Mesh
from jax.sharding import PartitionSpec as P

MODEL_WIDTH = 6144
HALF = 3072
GROUP = 6
HD = 128
CTX = 128
ROWS = 4
LOCAL_HEADS = 4
EXPERTS = 8
CAP = 2
HIDDEN = 512
AXES = ("role", "expert", "x", "y")
ORDER = (2, 1, -1)
SHIFTS = (0,) + ORDER
VMEM_SPEC = pl.BlockSpec(memory_space=pltpu.VMEM)
HBM_SPEC = pl.BlockSpec(memory_space=pltpu.HBM)
F32 = jnp.float32
BF16 = jnp.bfloat16


def call(body, out_shape, in_specs, flops=0, nbytes=0, scratch=()):
    single = not isinstance(out_shape, (tuple, list))
    out_specs = VMEM_SPEC if single else [VMEM_SPEC] * len(out_shape)
    return pl.pallas_call(
        body,
        out_shape=out_shape,
        in_specs=in_specs,
        out_specs=out_specs,
        scratch_shapes=list(scratch),
        compiler_params=pltpu.CompilerParams(vmem_limit_bytes=16 * 1024 * 1024),
        cost_estimate=pl.CostEstimate(flops=flops, bytes_accessed=nbytes, transcendentals=0),
    )


def in_hbm(value):
    return pltpu.with_memory_space_constraint(value, pltpu.HBM)


def attend_body(
    len_hbm, ids_hbm, logit_hbm, q_hbm, new_hbm, kv_hbm, res_hbm,
    hidden_ref, out_ref, comb_ref,
    len_ref, ids_ref, logit_ref, q_ref, new_ref, k_ref, v_ref, res_ref, sems,
):
    pairs = (
        (kv_hbm.at[:, 0], k_ref),
        (q_hbm, q_ref),
        (len_hbm, len_ref),
        (new_hbm, new_ref),
        (kv_hbm.at[:, 1], v_ref),
        (res_hbm, res_ref),
        (ids_hbm, ids_ref),
        (logit_hbm, logit_ref),
    )
    copies = [pltpu.make_async_copy(a, b, sems.at[i]) for i, (a, b) in enumerate(pairs)]
    for c in copies:
        c.start()
    scale = 1.0 / HD**0.5
    m_rows = GROUP * ROWS
    nt = (((1,), (1,)), ((), ()))
    for c in copies[:4]:
        c.wait()
    row_req = lax.broadcasted_iota(jnp.int32, (m_rows, 1), 0) % ROWS
    row_len = jnp.zeros((m_rows, 1), jnp.int32)
    for r in range(ROWS):
        row_len = jnp.where(row_req == r, len_ref[r], row_len)
    col = lax.broadcasted_iota(jnp.int32, (m_rows, ROWS * CTX), 1)
    valid = (col // CTX == row_req) & (col % CTX < row_len)
    own_valid = lax.broadcasted_iota(jnp.int32, (m_rows, ROWS), 1) == row_req
    new = new_ref[...].astype(F32)
    scores, owns = [], []
    for k in range(LOCAL_HEADS):
        sl = slice(k * HD, (k + 1) * HD)
        q = jnp.concatenate(
            [
                q_ref[:, (k * GROUP + g) * HD : (k * GROUP + g + 1) * HD].astype(F32)
                for g in range(GROUP)
            ],
            axis=0,
        ).astype(BF16)
        keys = k_ref[:, :, sl].reshape(ROWS * CTX, HD)
        nk = new[:, 0, sl].astype(BF16)
        s = lax.dot_general(q, keys, nt, preferred_element_type=F32) * scale
        so = lax.dot_general(q, nk, nt, preferred_element_type=F32) * scale
        scores.append(jnp.where(valid, s, -jnp.inf))
        owns.append(jnp.where(own_valid, so, -jnp.inf))
    tops = [
        jnp.maximum(jnp.max(s, axis=1, keepdims=True), jnp.max(so, axis=1, keepdims=True))
        for s, so in zip(scores, owns)
    ]
    es = [jnp.exp(s - t) for s, t in zip(scores, tops)]
    eos = [jnp.exp(so - t) for so, t in zip(owns, tops)]
    totals = [
        jnp.sum(e, axis=1, keepdims=True) + jnp.sum(eo, axis=1, keepdims=True)
        for e, eo in zip(es, eos)
    ]
    for c in copies[4:]:
        c.wait()
    for k in range(LOCAL_HEADS):
        sl = slice(k * HD, (k + 1) * HD)
        vals = v_ref[:, :, sl].reshape(ROWS * CTX, HD)
        nv = new[:, 1, sl].astype(BF16)
        p = (es[k] / totals[k]).astype(BF16)
        po = (eos[k] / totals[k]).astype(BF16)
        attn = jnp.dot(p, vals, preferred_element_type=F32) + jnp.dot(
            po, nv, preferred_element_type=F32
        )
        for g in range(GROUP):
            h = k * GROUP + g
            hs = slice(h * HD, (h + 1) * HD)
            hidden_ref[:, hs] = (
                res_ref[:, hs].astype(F32) + attn[g * ROWS : (g + 1) * ROWS]
            ).astype(BF16)
    ids = [ids_ref[p % 2, p // 2] for p in range(2 * ROWS)]
    rows = slot_rows(ids)
    ri = lax.broadcasted_iota(jnp.int32, (EXPERTS * CAP, ROWS), 0)
    ci = lax.broadcasted_iota(jnp.int32, (EXPERTS * CAP, ROWS), 1)
    select = jnp.zeros((EXPERTS * CAP, ROWS), F32)
    for p in range(2 * ROWS):
        select = jnp.where((ri == rows[p]) & (ci == p // 2), 1.0, select)
    out = jnp.dot(select.astype(BF16), hidden_ref[...], preferred_element_type=F32).astype(BF16)
    for e in range(EXPERTS):
        for a in range(2):
            out_ref[a * EXPERTS + e] = out[e * CAP : (e + 1) * CAP]
    lane = lax.broadcasted_iota(jnp.int32, (ROWS, HD), 1)
    tok = lax.broadcasted_iota(jnp.int32, (ROWS, HD), 0)
    diff = jnp.zeros((ROWS, HD), F32)
    for t in range(ROWS):
        gap = logit_ref[t, ids[2 * t]] - logit_ref[t, ids[2 * t + 1]]
        diff = jnp.where(tok == t, gap, diff)
    wa, wb = jax.nn.sigmoid(diff), jax.nn.sigmoid(-diff)
    place = lane % (EXPERTS * CAP)
    comb = jnp.zeros((ROWS, HD), F32)
    for t in range(ROWS):
        comb = jnp.where((tok == t) & (place == rows[2 * t]), wa, comb)
        comb = jnp.where((tok == t) & (place == rows[2 * t + 1]), wb, comb)
    high = comb.astype(BF16).astype(F32)
    mid = (comb - high).astype(BF16).astype(F32)
    low = comb - high - mid
    comb_ref[...] = jnp.concatenate([high, mid, low, jnp.zeros_like(low)], axis=0).astype(BF16)


def slot_rows(ids):
    rows = []
    for p in range(len(ids)):
        slot = jnp.int32(0)
        for q in range(p):
            slot = slot + (ids[q] == ids[p]).astype(jnp.int32)
        rows.append(ids[p] * CAP + slot)
    return rows


CHUNK = 768
PART = 32


def scale_rows(x_ref, gain, scaled_ref, at, sq_ref, send_ref):
    lane = lax.broadcasted_iota(jnp.int32, (PART, HD), 1)
    acc = jnp.zeros((PART, HD), F32)
    for c in range(0, HALF, HD):
        part = x_ref[:, c : c + HD].astype(F32)
        acc = acc + part * part
        scaled_ref[at : at + PART, c : c + HD] = (part * gain(c)).astype(BF16)
    total = jnp.broadcast_to(jnp.sum(acc, axis=1, keepdims=True), (PART, HD))
    high = total.astype(BF16).astype(F32)
    low = jnp.where(high < jnp.inf, total - high, 0.0)
    sq_ref[at : at + PART] = total
    send_ref[at : at + PART, 2 * HIDDEN :] = jnp.where(lane < HD // 2, high, low).astype(BF16)


def first_body(*refs):
    xs, (gain_hbm, wg_hbm, wu_hbm, wd_hbm) = refs[:5], refs[5:9]
    own_ref, sq_ref, send_ref, gain_out, wg_ref, wu_ref, wd_ref = refs[9:16]
    gain_ref, scaled_ref, sems = refs[16:]
    steps = [(k, w) for k in range(0, HALF, CHUNK) for w in (0, 1)]
    sources, targets = (wg_hbm, wu_hbm), (wg_ref, wu_ref)

    def fetch(n):
        k, w = steps[n]
        rows = pl.ds(k, CHUNK)
        return pltpu.make_async_copy(sources[w].at[0, rows], targets[w].at[rows], sems.at[n])

    count = len(steps)
    gain_copy = pltpu.make_async_copy(gain_hbm, gain_ref, sems.at[count])
    down_copy = pltpu.make_async_copy(wd_hbm.at[0], wd_ref, sems.at[count + 1])
    gain_copy.start()
    for n in range(count):
        fetch(n).start()
    down_copy.start()
    gain_copy.wait()
    for c in range(0, HALF, HD):
        gain_out[:, c : c + HD] = gain_ref[pl.ds(c, HD)].astype(F32).reshape(1, HD)
    for n, x_ref in enumerate(xs):
        scale_rows(
            x_ref, lambda c: gain_out[:, c : c + HD], scaled_ref, n * PART, sq_ref, send_ref
        )
    for n, (k, w) in enumerate(steps):
        fetch(n).wait()
        rows = slice(k, k + CHUNK)
        at = slice(w * HIDDEN, (w + 1) * HIDDEN)
        got = jnp.dot(scaled_ref[:, rows], targets[w][rows], preferred_element_type=F32)
        if k:
            got = got + own_ref[:, at]
        own_ref[:, at] = got
        if k + CHUNK == HALF:
            send_ref[:, at] = got.astype(BF16)
    down_copy.wait()


def second_body(*refs):
    xs, (gain_ref, wg_ref, wu_ref) = refs[:3], refs[3:6]
    own_ref, sq_ref, send_ref, scaled_ref = refs[6:]
    for n, x_ref in enumerate(xs):
        scale_rows(
            x_ref, lambda c: gain_ref[:, c : c + HD], scaled_ref, n * PART, sq_ref, send_ref
        )
    x = scaled_ref[...]
    for at, w_ref in ((0, wg_ref), (HIDDEN, wu_ref)):
        got = jnp.dot(x, w_ref[...], preferred_element_type=F32)
        own_ref[:, at : at + HIDDEN] = got
        send_ref[:, at : at + HIDDEN] = got.astype(BF16)


def coordinates():
    role, x, y = (lax.axis_index(n) for n in ("role", "x", "y"))
    return jnp.where(role == 0, x, y), jnp.where(role == 0, y, x)


def down_body(own0, sq0, own1, sq1, got0, got1, wd_ref, *rest):
    outs, (act_ref, got_ref) = rest[:8], rest[8:]
    early = got0.shape[0]
    got_ref[:early] = got0[...]
    got_ref[early:] = got1[...]
    my_a, my_b = coordinates()
    for jp in range(2):
        for jb in range(4):
            for ai in range(2):
                at = (jp * 8 + jb * 2 + ai) * 16
                ours, sqs, mine = (own0, sq0, at) if at < early else (own1, sq1, at - early)
                away = lax.rem(my_a - 2 * lax.rem(my_a // 2 + jp, 2) - ai + 4, 4)
                peer_b = jnp.where(away == 2, 1, jnp.where(away == 1, 2, away))
                peer_a = lax.rem(my_b - SHIFTS[jb] + 4, 4)
                peer_p = lax.rem(peer_a // 2 + my_b // 2, 2)
                peer = (peer_p * 8 + peer_b * 2 + lax.rem(peer_a, 2)) * 16
                got = got_ref[pl.ds(pl.multiple_of(peer, 16), 16)].astype(F32)
                lane = 2 * HIDDEN
                extra = got[:, lane : lane + 1] + got[:, lane + HD // 2 : lane + HD // 2 + 1]
                total = sqs[mine : mine + 16][:, :1] + extra
                inv = lax.rsqrt(total / MODEL_WIDTH + 1e-05)
                pre = ours[mine : mine + 16] + got[:, : 2 * HIDDEN]
                pre = jnp.where(inv > 0.0, pre * inv, 0.0)
                gate = pre[:, :HIDDEN]
                act = gate * jax.nn.sigmoid(gate) * pre[:, HIDDEN:]
                act_ref[at : at + 16] = act.astype(BF16)
    act = act_ref[...]
    for n in range(0, HALF, 512):
        got = jnp.dot(act, wd_ref[:, n : n + 512], preferred_element_type=F32).astype(BF16)
        for j in range(8):
            outs[j][:, n : n + 512] = got[j * PART : (j + 1) * PART]


def sum_body(*refs):
    total = refs[0][...].astype(F32)
    for r in refs[1:-1]:
        total = total + r[...].astype(F32)
    refs[-1][...] = total.astype(BF16)


def combine_body(comb_ref, hidden_ref, back_ref, out_ref):
    got = jnp.dot(comb_ref[:, :PART], back_ref[...], preferred_element_type=F32)
    moe = got[:ROWS] + got[ROWS : 2 * ROWS] + got[2 * ROWS : 3 * ROWS]
    out_ref[...] = (hidden_ref[...].astype(F32) + moe).astype(BF16)


def index_of(role, z, x, y):
    return ((role * 8 + z) * 4 + x) * 4 + y


def permutation(move):
    return [
        (index_of(r, z, x, y), index_of(*move(r, z, x, y)))
        for r in range(2)
        for z in range(8)
        for x in range(4)
        for y in range(4)
    ]


def along_x(s, r, z, x, y):
    return r, z, (x + s) % 4, y


def along_y(s, r, z, x, y):
    return r, z, x, (y + s) % 4


def send_b(value, s):
    return lax.ppermute(
        value,
        AXES,
        permutation(lambda r, z, x, y: along_y(s, r, z, x, y) if r == 0 else along_x(s, r, z, x, y)),
    )


def send_a(value):
    return lax.ppermute(
        value,
        AXES,
        permutation(lambda r, z, x, y: along_x(2, r, z, x, y) if r == 0 else along_y(2, r, z, x, y)),
    )


def swap(value):
    return lax.ppermute(value, "role", [(0, 1), (1, 0)])


def exchange(value):
    groups = []
    for p in (0, 2):
        for o in range(4):
            pair = [(a, z) for a in (p, p + 1) for z in range(8)]
            groups.append([index_of(0, z, a, o) for a, z in pair])
            groups.append([index_of(1, z, o, a) for a, z in pair])
    return lax.all_to_all(
        value, AXES, split_axis=0, concat_axis=0, axis_index_groups=groups, tiled=True
    )


def per_device(
    query, new_kv, kv_cache, lengths, residual, norm_gain, expert_ids, router_logits, w_gate, w_up, w_down
):
    shape = jax.ShapeDtypeStruct
    hidden, outgoing, comb = call(
        attend_body,
        (shape((ROWS, HALF), BF16), shape((2 * EXPERTS, CAP, HALF), BF16), shape((4 * ROWS, HD), BF16)),
        [HBM_SPEC] * 7,
        flops=50_000_000,
        nbytes=1_200_000,
        scratch=[
            pltpu.SMEM((ROWS,), jnp.int32),
            pltpu.SMEM((2, ROWS), jnp.int32),
            pltpu.SMEM((ROWS, EXPERTS), F32),
            pltpu.VMEM((ROWS, HALF), BF16),
            pltpu.VMEM((ROWS, 2, HIDDEN), BF16),
            pltpu.VMEM((ROWS, CTX, HIDDEN), BF16),
            pltpu.VMEM((ROWS, CTX, HIDDEN), BF16),
            pltpu.VMEM((ROWS, HALF), BF16),
            pltpu.SemaphoreType.DMA((8,)),
        ],
    )(*map(in_hbm, (lengths, expert_ids.T, router_logits, query, new_kv, kv_cache, residual)))
    near = exchange(outgoing).reshape(PART, HALF)
    far = send_a(near)
    near_b = [send_b(near, s) for s in ORDER]
    far_b = [send_b(far, s) for s in ORDER]

    def partials(rows):
        return (
            shape((rows, 2 * HIDDEN), F32),
            shape((rows, HD), F32),
            shape((rows, 2 * HIDDEN + HD), BF16),
        )

    own0, sq0, send0, gain, wg, wu, wd = call(
        first_body,
        partials(5 * PART)
        + (
            shape((1, HALF), F32),
            pltpu.VMEM((HALF, HIDDEN), BF16),
            pltpu.VMEM((HALF, HIDDEN), BF16),
            pltpu.VMEM((HIDDEN, HALF), BF16),
        ),
        [VMEM_SPEC] * 5 + [HBM_SPEC] * 4,
        flops=2 * 5 * PART * HALF * 1024,
        nbytes=20_000_000,
        scratch=[
            pltpu.VMEM((HALF,), BF16),
            pltpu.VMEM((5 * PART, HALF), BF16),
            pltpu.SemaphoreType.DMA((2 * HALF // CHUNK + 2,)),
        ],
    )(near, *near_b, far, *map(in_hbm, (norm_gain, w_gate, w_up, w_down)))
    own1, sq1, send1 = call(
        second_body,
        partials(3 * PART),
        [VMEM_SPEC] * 6,
        flops=2 * 3 * PART * HALF * 1024,
        nbytes=8_000_000,
        scratch=[pltpu.VMEM((3 * PART, HALF), BF16)],
    )(*far_b, gain, wg, wu)
    terms = call(
        down_body,
        [shape((PART, HALF), BF16)] * 8,
        [VMEM_SPEC] * 7,
        flops=2 * 256 * HALF * 512,
        nbytes=6_000_000,
        scratch=[pltpu.VMEM((256, HIDDEN), BF16), pltpu.VMEM((256, 2 * HIDDEN + HD), BF16)],
    )(own0, sq0, own1, sq1, swap(send0), swap(send1), wd)

    def add_up(parts):
        return call(
            sum_body,
            shape((PART, HALF), BF16),
            [VMEM_SPEC] * len(parts),
            flops=400_000,
            nbytes=1_000_000,
        )(*parts)

    far_sum = add_up([terms[4]] + [send_b(terms[4 + j], -SHIFTS[j]) for j in (1, 2, 3)])
    near_got = [send_b(terms[j], -SHIFTS[j]) for j in (1, 2, 3)]
    summed = add_up([terms[0]] + near_got + [send_a(far_sum)])
    back = exchange(summed.reshape(2 * EXPERTS, CAP, HALF)).reshape(PART, HALF)
    return call(
        combine_body,
        shape((ROWS, HALF), BF16),
        [VMEM_SPEC] * 3,
        flops=100_000,
        nbytes=150_000,
    )(comb, hidden, back)


def solution(mesh):
    fine = Mesh(mesh.devices.reshape(2, 8, 4, 4), AXES)
    rows = ("expert", "x", "y")
    shard = ("x", "y")
    in_specs = (
        P(rows, "role"),
        P(rows, None, "role"),
        P(rows, None, None, "role"),
        P(rows),
        P(rows, "role"),
        P("role"),
        P(rows, None),
        P(rows, None),
        P("expert", "role", shard),
        P("expert", "role", shard),
        P("expert", shard, "role"),
    )
    return jax.shard_map(
        per_device, mesh=fine, in_specs=in_specs, out_specs=P(rows, "role"), check_vma=False
    )
```

```python
import functools

import jax
import jax.numpy as jnp
from jax import lax
from jax.experimental import pallas as pl
from jax.experimental.pallas import tpu as pltpu
from jax.sharding import Mesh
from jax.sharding import PartitionSpec as P

MODEL_WIDTH = 6144
HALF = 3072
GROUP = 6
HD = 128
CTX = 128
ROWS = 4
LOCAL_HEADS = 4
EXPERTS = 8
CAP = 2
HIDDEN = 512
AXES = ("role", "expert", "x", "y")
ORDER = (2, 1, -1)
SHIFTS = (0,) + ORDER
VMEM_SPEC = pl.BlockSpec(memory_space=pltpu.VMEM)
HBM_SPEC = pl.BlockSpec(memory_space=pltpu.HBM)
F32 = jnp.float32
BF16 = jnp.bfloat16


def call(body, out_shape, in_specs, flops=0, nbytes=0, scratch=(), aliases=None):
    single = not isinstance(out_shape, (tuple, list))
    out_specs = VMEM_SPEC if single else [VMEM_SPEC] * len(out_shape)
    return pl.pallas_call(
        body,
        out_shape=out_shape,
        in_specs=in_specs,
        out_specs=out_specs,
        scratch_shapes=list(scratch),
        input_output_aliases=aliases or {},
        compiler_params=pltpu.CompilerParams(vmem_limit_bytes=16 * 1024 * 1024),
        cost_estimate=pl.CostEstimate(flops=flops, bytes_accessed=nbytes, transcendentals=0),
    )


def in_hbm(value):
    return pltpu.with_memory_space_constraint(value, pltpu.HBM)


def attend_body(
    len_hbm, ids_hbm, logit_hbm, q_hbm, new_hbm, kv_hbm, res_hbm, gain_hbm,
    hidden_ref, out_ref, comb_ref, gain_out,
    len_ref, ids_ref, logit_ref, q_ref, new_ref, k_ref, v_ref, res_ref, gain_ref, sems,
):
    pairs = (
        (kv_hbm.at[:, 0], k_ref),
        (q_hbm, q_ref),
        (len_hbm, len_ref),
        (new_hbm, new_ref),
        (kv_hbm.at[:, 1], v_ref),
        (res_hbm, res_ref),
        (ids_hbm, ids_ref),
        (logit_hbm, logit_ref),
        (gain_hbm, gain_ref),
    )
    copies = [pltpu.make_async_copy(a, b, sems.at[i]) for i, (a, b) in enumerate(pairs)]
    for c in copies:
        c.start()
    scale = 1.0 / HD**0.5
    m_rows = GROUP * ROWS
    nt = (((1,), (1,)), ((), ()))
    for c in copies[:4]:
        c.wait()
    row_req = lax.broadcasted_iota(jnp.int32, (m_rows, 1), 0) % ROWS
    row_len = jnp.zeros((m_rows, 1), jnp.int32)
    for r in range(ROWS):
        row_len = jnp.where(row_req == r, len_ref[r], row_len)
    col = lax.broadcasted_iota(jnp.int32, (m_rows, ROWS * CTX), 1)
    valid = (col // CTX == row_req) & (col % CTX < row_len)
    own_valid = lax.broadcasted_iota(jnp.int32, (m_rows, ROWS), 1) == row_req
    new = new_ref[...].astype(F32)
    scores, owns = [], []
    for k in range(LOCAL_HEADS):
        sl = slice(k * HD, (k + 1) * HD)
        q = jnp.concatenate(
            [
                q_ref[:, (k * GROUP + g) * HD : (k * GROUP + g + 1) * HD].astype(F32)
                for g in range(GROUP)
            ],
            axis=0,
        ).astype(BF16)
        keys = k_ref[:, :, sl].reshape(ROWS * CTX, HD)
        nk = new[:, 0, sl].astype(BF16)
        s = lax.dot_general(q, keys, nt, preferred_element_type=F32) * scale
        so = lax.dot_general(q, nk, nt, preferred_element_type=F32) * scale
        scores.append(jnp.where(valid, s, -jnp.inf))
        owns.append(jnp.where(own_valid, so, -jnp.inf))
    tops = [
        jnp.maximum(jnp.max(s, axis=1, keepdims=True), jnp.max(so, axis=1, keepdims=True))
        for s, so in zip(scores, owns)
    ]
    es = [jnp.exp(s - t) for s, t in zip(scores, tops)]
    eos = [jnp.exp(so - t) for so, t in zip(owns, tops)]
    totals = [
        jnp.sum(e, axis=1, keepdims=True) + jnp.sum(eo, axis=1, keepdims=True)
        for e, eo in zip(es, eos)
    ]
    for c in copies[4:]:
        c.wait()
    for k in range(LOCAL_HEADS):
        sl = slice(k * HD, (k + 1) * HD)
        vals = v_ref[:, :, sl].reshape(ROWS * CTX, HD)
        nv = new[:, 1, sl].astype(BF16)
        p = (es[k] / totals[k]).astype(BF16)
        po = (eos[k] / totals[k]).astype(BF16)
        attn = jnp.dot(p, vals, preferred_element_type=F32) + jnp.dot(
            po, nv, preferred_element_type=F32
        )
        for g in range(GROUP):
            h = k * GROUP + g
            hs = slice(h * HD, (h + 1) * HD)
            hidden_ref[:, hs] = (
                res_ref[:, hs].astype(F32) + attn[g * ROWS : (g + 1) * ROWS]
            ).astype(BF16)
    for c in range(0, HALF, HD):
        gain_out[:, c : c + HD] = gain_ref[pl.ds(c, HD)].astype(F32).reshape(1, HD)
    ids = [ids_ref[p % 2, p // 2] for p in range(2 * ROWS)]
    rows = slot_rows(ids)
    ri = lax.broadcasted_iota(jnp.int32, (EXPERTS * CAP, ROWS), 0)
    ci = lax.broadcasted_iota(jnp.int32, (EXPERTS * CAP, ROWS), 1)
    select = jnp.zeros((EXPERTS * CAP, ROWS), F32)
    for p in range(2 * ROWS):
        select = jnp.where((ri == rows[p]) & (ci == p // 2), 1.0, select)
    out = jnp.dot(select.astype(BF16), hidden_ref[...], preferred_element_type=F32).astype(BF16)
    for e in range(EXPERTS):
        for a in range(2):
            out_ref[a * EXPERTS + e] = out[e * CAP : (e + 1) * CAP]
    lane = lax.broadcasted_iota(jnp.int32, (ROWS, HD), 1)
    tok = lax.broadcasted_iota(jnp.int32, (ROWS, HD), 0)
    diff = jnp.zeros((ROWS, HD), F32)
    for t in range(ROWS):
        gap = logit_ref[t, ids[2 * t]] - logit_ref[t, ids[2 * t + 1]]
        diff = jnp.where(tok == t, gap, diff)
    wa, wb = jax.nn.sigmoid(diff), jax.nn.sigmoid(-diff)
    place = lane % (EXPERTS * CAP)
    comb = jnp.zeros((ROWS, HD), F32)
    for t in range(ROWS):
        comb = jnp.where((tok == t) & (place == rows[2 * t]), wa, comb)
        comb = jnp.where((tok == t) & (place == rows[2 * t + 1]), wb, comb)
    high = comb.astype(BF16).astype(F32)
    mid = (comb - high).astype(BF16).astype(F32)
    low = comb - high - mid
    comb_ref[...] = jnp.concatenate([high, mid, low, jnp.zeros_like(low)], axis=0).astype(BF16)


def slot_rows(ids):
    rows = []
    for p in range(len(ids)):
        slot = jnp.int32(0)
        for q in range(p):
            slot = slot + (ids[q] == ids[p]).astype(jnp.int32)
        rows.append(ids[p] * CAP + slot)
    return rows


CHUNK = 768
PART = 32


def scale_rows(x_ref, gain_ref, scaled_ref, at, cols, acc):
    for c in range(cols.start, cols.stop, HD):
        part = x_ref[:, c : c + HD].astype(F32)
        acc = acc + part * part
        scaled_ref[at : at + PART, c : c + HD] = (part * gain_ref[:, c : c + HD]).astype(BF16)
    return acc


def put_squares(acc, at, sq_ref, send_ref):
    lane = lax.broadcasted_iota(jnp.int32, (PART, HD), 1)
    total = jnp.broadcast_to(jnp.sum(acc, axis=1, keepdims=True), (PART, HD))
    high = total.astype(BF16).astype(F32)
    low = jnp.where(high < jnp.inf, total - high, 0.0)
    sq_ref[at : at + PART] = total
    send_ref[at : at + PART, 2 * HIDDEN :] = jnp.where(lane < HD // 2, high, low).astype(BF16)


def gate_up(xs, gain_ref, wg_ref, wu_ref, own_ref, sq_ref, send_ref, scaled_ref, chunk):
    accs = [jnp.zeros((PART, HD), F32) for _ in xs]
    sums = [None, None]
    for k in range(0, HALF, chunk):
        rows = slice(k, k + chunk)
        for n, x_ref in enumerate(xs):
            accs[n] = scale_rows(x_ref, gain_ref, scaled_ref, n * PART, rows, accs[n])
        x = scaled_ref[:, rows]
        for i, w_ref in enumerate((wg_ref, wu_ref)):
            got = jnp.dot(x, w_ref[rows], preferred_element_type=F32)
            sums[i] = got if sums[i] is None else sums[i] + got
    for i, at in enumerate((0, HIDDEN)):
        own_ref[:, at : at + HIDDEN] = sums[i]
        send_ref[:, at : at + HIDDEN] = sums[i].astype(BF16)
    for n in range(len(xs)):
        put_squares(accs[n], n * PART, sq_ref, send_ref)


def weight_copies(sources, targets, sems):
    steps = [(k, w) for k in range(0, HALF, CHUNK) for w in (0, 1)]
    copies = []
    for n, (k, w) in enumerate(steps):
        rows = pl.ds(k, CHUNK)
        copies.append(
            pltpu.make_async_copy(sources[w].at[0, rows], targets[w].at[rows], sems.at[n])
        )
    return steps, copies


def ahead_body(after_ref, wg_hbm, wu_hbm, wg_ref, wu_ref, sems):
    del after_ref

    @pl.when(lax.axis_index("role") == 1)
    def _():
        _, copies = weight_copies((wg_hbm, wu_hbm), (wg_ref, wu_ref), sems)
        for c in copies:
            c.start()
        for c in copies:
            c.wait()


def first_body(*refs):
    xs, gain_ref, sources = refs[:5], refs[5], refs[6:8]
    own_ref, sq_ref, send_ref, wg_ref, wu_ref = refs[10:15]
    scaled_ref, sems = refs[15:]
    late = lax.axis_index("role") == 0
    targets = (wg_ref, wu_ref)
    steps, copies = weight_copies(sources, targets, sems)

    @pl.when(late)
    def _():
        for c in copies:
            c.start()

    @pl.when(late)
    def _():
        for n, x_ref in enumerate(xs):
            zero = jnp.zeros((PART, HD), F32)
            acc = scale_rows(x_ref, gain_ref, scaled_ref, n * PART, slice(0, HALF), zero)
            put_squares(acc, n * PART, sq_ref, send_ref)
        for n, (k, w) in enumerate(steps):
            copies[n].wait()
            rows = slice(k, k + CHUNK)
            at = slice(w * HIDDEN, (w + 1) * HIDDEN)
            got = jnp.dot(scaled_ref[:, rows], targets[w][rows], preferred_element_type=F32)
            if k:
                got = got + own_ref[:, at]
            own_ref[:, at] = got
            if k + CHUNK == HALF:
                send_ref[:, at] = got.astype(BF16)
    @pl.when(jnp.logical_not(late))
    def _():
        gate_up(xs, gain_ref, wg_ref, wu_ref, own_ref, sq_ref, send_ref, scaled_ref, 2 * CHUNK)


def second_body(*refs):
    xs, (gain_ref, wg_ref, wu_ref) = refs[:3], refs[3:6]
    own_ref, sq_ref, send_ref, scaled_ref = refs[6:]
    gate_up(xs, gain_ref, wg_ref, wu_ref, own_ref, sq_ref, send_ref, scaled_ref, 2 * CHUNK)


def coordinates():
    role, x, y = (lax.axis_index(n) for n in ("role", "x", "y"))
    return jnp.where(role == 0, y, x), jnp.where(role == 0, x, y)


def down_body(blocks, splits, own0, sq0, own1, sq1, got0, got1, wd_ref, *rest):
    outs, (act_ref, got_ref) = rest[: len(splits)], rest[len(splits) :]
    early = got0.shape[0]
    got_ref[:early] = got0[...]
    got_ref[early:] = got1[...]
    my_a, my_b = coordinates()
    for n, (jp, jb) in enumerate(blocks):
        for ai in range(2):
            at = (jp * 8 + jb * 2 + ai) * 16
            ours, sqs, mine = (own0, sq0, at) if at < early else (own1, sq1, at - early)
            away = lax.rem(my_a - 2 * lax.rem(my_a // 2 + jp, 2) - ai + 4, 4)
            peer_b = jnp.where(away == 2, 1, jnp.where(away == 1, 2, away))
            peer_a = lax.rem(my_b - SHIFTS[jb] + 4, 4)
            peer_p = lax.rem(peer_a // 2 + my_b // 2, 2)
            peer = (peer_p * 8 + peer_b * 2 + lax.rem(peer_a, 2)) * 16
            got = got_ref[pl.ds(pl.multiple_of(peer, 16), 16)].astype(F32)
            lane = 2 * HIDDEN
            extra = got[:, lane : lane + 1] + got[:, lane + HD // 2 : lane + HD // 2 + 1]
            total = sqs[mine : mine + 16][:, :1] + extra
            inv = lax.rsqrt(total / MODEL_WIDTH + 1e-05)
            pre = ours[mine : mine + 16] + got[:, : 2 * HIDDEN]
            pre = jnp.where(inv > 0.0, pre * inv, 0.0)
            gate = pre[:, :HIDDEN]
            act = gate * jax.nn.sigmoid(gate) * pre[:, HIDDEN:]
            act_ref[(n * 2 + ai) * 16 : (n * 2 + ai + 1) * 16] = act.astype(BF16)
    act = act_ref[...]
    for c in range(0, HALF, 512):
        got = jnp.dot(act, wd_ref[:, c : c + 512], preferred_element_type=F32).astype(BF16)
        start = 0
        for out_ref, rows in zip(outs, splits):
            out_ref[:, c : c + 512] = got[start : start + rows]
            start += rows


def sum_body(*refs):
    total = refs[0][...].astype(F32)
    for r in refs[1:-1]:
        total = total + r[...].astype(F32)
    refs[-1][...] = total.astype(BF16)


def combine_body(comb_ref, hidden_ref, back_ref, out_ref):
    got = jnp.dot(comb_ref[:, :PART], back_ref[...], preferred_element_type=F32)
    moe = got[:ROWS] + got[ROWS : 2 * ROWS] + got[2 * ROWS : 3 * ROWS]
    out_ref[...] = (hidden_ref[...].astype(F32) + moe).astype(BF16)


def index_of(role, z, x, y):
    return ((role * 8 + z) * 4 + x) * 4 + y


def permutation(move):
    return [
        (index_of(r, z, x, y), index_of(*move(r, z, x, y)))
        for r in range(2)
        for z in range(8)
        for x in range(4)
        for y in range(4)
    ]


def along_x(s, r, z, x, y):
    return r, z, (x + s) % 4, y


def along_y(s, r, z, x, y):
    return r, z, x, (y + s) % 4


def send_b(value, s):
    return lax.ppermute(
        value,
        AXES,
        permutation(lambda r, z, x, y: along_x(s, r, z, x, y) if r == 0 else along_y(s, r, z, x, y)),
    )


def send_a(value):
    return lax.ppermute(
        value,
        AXES,
        permutation(lambda r, z, x, y: along_y(2, r, z, x, y) if r == 0 else along_x(2, r, z, x, y)),
    )


def swap(value):
    return lax.ppermute(value, "role", [(0, 1), (1, 0)])


def exchange(value):
    groups = []
    for p in (0, 2):
        for o in range(4):
            pair = [(a, z) for a in (p, p + 1) for z in range(8)]
            groups.append([index_of(0, z, o, a) for a, z in pair])
            groups.append([index_of(1, z, a, o) for a, z in pair])
    return lax.all_to_all(
        value, AXES, split_axis=0, concat_axis=0, axis_index_groups=groups, tiled=True
    )


def per_device(
    query, new_kv, kv_cache, lengths, residual, norm_gain, expert_ids, router_logits, w_gate, w_up, w_down
):
    shape = jax.ShapeDtypeStruct
    hidden, outgoing, comb, gain = call(
        attend_body,
        (shape((ROWS, HALF), BF16), shape((2 * EXPERTS, CAP, HALF), BF16), shape((4 * ROWS, HD), BF16), shape((1, HALF), F32)),
        [HBM_SPEC] * 8,
        flops=50_000_000,
        nbytes=1_200_000,
        scratch=[
            pltpu.SMEM((ROWS,), jnp.int32),
            pltpu.SMEM((2, ROWS), jnp.int32),
            pltpu.SMEM((ROWS, EXPERTS), F32),
            pltpu.VMEM((ROWS, HALF), BF16),
            pltpu.VMEM((ROWS, 2, HIDDEN), BF16),
            pltpu.VMEM((ROWS, CTX, HIDDEN), BF16),
            pltpu.VMEM((ROWS, CTX, HIDDEN), BF16),
            pltpu.VMEM((ROWS, HALF), BF16),
            pltpu.VMEM((HALF,), BF16),
            pltpu.SemaphoreType.DMA((9,)),
        ],
    )(*map(in_hbm, (lengths, expert_ids.T, router_logits, query, new_kv, kv_cache, residual, norm_gain)))
    near = exchange(outgoing).reshape(PART, HALF)
    far = send_a(near)
    blocks = (
        pltpu.VMEM((HALF, HIDDEN), BF16),
        pltpu.VMEM((HALF, HIDDEN), BF16),
    )
    count = 2 * HALF // CHUNK
    sources = tuple(map(in_hbm, (w_gate, w_up)))
    ahead = call(
        ahead_body,
        blocks,
        [VMEM_SPEC] + [HBM_SPEC] * 2,
        nbytes=12_000_000,
        scratch=[pltpu.SemaphoreType.DMA((count,))],
    )(near, *sources)
    near, *ahead = lax.optimization_barrier((near, *ahead))
    near_b = [send_b(near, s) for s in ORDER]
    far_b = [send_b(far, s) for s in ORDER]

    def partials(rows):
        return (
            shape((rows, 2 * HIDDEN), F32),
            shape((rows, HD), F32),
            shape((rows, 2 * HIDDEN + HD), BF16),
        )

    own0, sq0, send0, wg, wu = call(
        first_body,
        partials(5 * PART) + blocks,
        [VMEM_SPEC] * 6 + [HBM_SPEC] * 2 + [VMEM_SPEC] * 2,
        flops=2 * 5 * PART * HALF * 1024,
        nbytes=20_000_000,
        scratch=[
            pltpu.VMEM((5 * PART, HALF), BF16),
            pltpu.SemaphoreType.DMA((count,)),
        ],
        aliases={8: 3, 9: 4},
    )(near, *near_b, far, gain, *sources, *ahead)
    own1, sq1, send1 = call(
        second_body,
        partials(3 * PART),
        [VMEM_SPEC] * 6,
        flops=2 * 3 * PART * HALF * 1024,
        nbytes=8_000_000,
        scratch=[pltpu.VMEM((3 * PART, HALF), BF16)],
    )(*far_b, gain, wg, wu)
    swapped0, swapped1 = swap(send0), swap(send1)

    def down(blocks, splits):
        rows = PART * len(blocks)
        return call(
            functools.partial(down_body, blocks, splits),
            [shape((n, HALF), BF16) for n in splits],
            [VMEM_SPEC] * 7,
            flops=2 * rows * HALF * 512,
            nbytes=5_000_000,
            scratch=[pltpu.VMEM((rows, HIDDEN), BF16), pltpu.VMEM((256, 2 * HIDDEN + HD), BF16)],
        )(own0, sq0, own1, sq1, swapped0, swapped1, w_down[0])

    far_terms = down(tuple((1, j) for j in range(4)), (PART,) * 4)
    near_terms = down(tuple((0, j) for j in range(4)), (PART,) * 4)

    def add_up(*parts):
        return call(
            sum_body,
            shape((PART, HALF), BF16),
            [VMEM_SPEC] * len(parts),
            flops=400_000,
            nbytes=1_000_000,
        )(*parts)

    far_sum = add_up(far_terms[0], *[send_b(far_terms[j], -SHIFTS[j]) for j in (1, 2, 3)])
    near_got = [send_b(near_terms[j], -SHIFTS[j]) for j in (2, 3, 1)]
    summed = add_up(near_terms[0], *near_got, send_a(far_sum))
    back = exchange(summed.reshape(2 * EXPERTS, CAP, HALF)).reshape(PART, HALF)
    return call(
        combine_body,
        shape((ROWS, HALF), BF16),
        [VMEM_SPEC] * 3,
        flops=100_000,
        nbytes=150_000,
    )(comb, hidden, back)


def solution(mesh):
    fine = Mesh(mesh.devices.reshape(2, 8, 4, 4), AXES)
    rows = ("expert", "x", "y")
    shard = ("x", "y")
    in_specs = (
        P(rows, "role"),
        P(rows, None, "role"),
        P(rows, None, None, "role"),
        P(rows),
        P(rows, "role"),
        P("role"),
        P(rows, None),
        P(rows, None),
        P("expert", "role", shard),
        P("expert", "role", shard),
        P("expert", shard, "role"),
    )
    return jax.shard_map(
        per_device, mesh=fine, in_specs=in_specs, out_specs=P(rows, "role"), check_vma=False
    )
```

```python
import functools

import jax
import jax.numpy as jnp
from jax import lax
from jax.experimental import pallas as pl
from jax.experimental.pallas import tpu as pltpu
from jax.sharding import Mesh
from jax.sharding import PartitionSpec as P

MODEL_WIDTH = 6144
HALF = 3072
GROUP = 6
HD = 128
CTX = 128
ROWS = 4
LOCAL_HEADS = 4
EXPERTS = 8
CAP = 2
HIDDEN = 512
AXES = ("role", "expert", "x", "y")
ORDER = (2, 1, -1)
SHIFTS = (0,) + ORDER
VMEM_SPEC = pl.BlockSpec(memory_space=pltpu.VMEM)
HBM_SPEC = pl.BlockSpec(memory_space=pltpu.HBM)
F32 = jnp.float32
BF16 = jnp.bfloat16


def call(body, out_shape, in_specs, flops=0, nbytes=0, scratch=(), aliases=None):
    single = not isinstance(out_shape, (tuple, list))
    out_specs = VMEM_SPEC if single else [VMEM_SPEC] * len(out_shape)
    return pl.pallas_call(
        body,
        out_shape=out_shape,
        in_specs=in_specs,
        out_specs=out_specs,
        scratch_shapes=list(scratch),
        input_output_aliases=aliases or {},
        compiler_params=pltpu.CompilerParams(vmem_limit_bytes=16 * 1024 * 1024),
        cost_estimate=pl.CostEstimate(flops=flops, bytes_accessed=nbytes, transcendentals=0),
    )


def in_hbm(value):
    return pltpu.with_memory_space_constraint(value, pltpu.HBM)


def attend_body(
    len_hbm, ids_hbm, logit_hbm, q_hbm, new_hbm, kv_hbm, res_hbm, gain_hbm,
    hidden_ref, out_ref, comb_ref, gain_out,
    len_ref, ids_ref, logit_ref, q_ref, new_ref, k_ref, v_ref, res_ref, gain_ref, sems,
):
    pairs = (
        (kv_hbm.at[:, 0], k_ref),
        (q_hbm, q_ref),
        (len_hbm, len_ref),
        (new_hbm, new_ref),
        (kv_hbm.at[:, 1], v_ref),
        (res_hbm, res_ref),
        (ids_hbm, ids_ref),
        (logit_hbm, logit_ref),
        (gain_hbm, gain_ref),
    )
    copies = [pltpu.make_async_copy(a, b, sems.at[i]) for i, (a, b) in enumerate(pairs)]
    for c in copies:
        c.start()
    scale = 1.0 / HD**0.5
    m_rows = GROUP * ROWS
    nt = (((1,), (1,)), ((), ()))
    for c in copies[:4]:
        c.wait()
    row_req = lax.broadcasted_iota(jnp.int32, (m_rows, 1), 0) % ROWS
    row_len = jnp.zeros((m_rows, 1), jnp.int32)
    for r in range(ROWS):
        row_len = jnp.where(row_req == r, len_ref[r], row_len)
    col = lax.broadcasted_iota(jnp.int32, (m_rows, ROWS * CTX), 1)
    valid = (col // CTX == row_req) & (col % CTX < row_len)
    own_valid = lax.broadcasted_iota(jnp.int32, (m_rows, ROWS), 1) == row_req
    new = new_ref[...].astype(F32)
    scores, owns = [], []
    for k in range(LOCAL_HEADS):
        sl = slice(k * HD, (k + 1) * HD)
        q = jnp.concatenate(
            [
                q_ref[:, (k * GROUP + g) * HD : (k * GROUP + g + 1) * HD].astype(F32)
                for g in range(GROUP)
            ],
            axis=0,
        ).astype(BF16)
        keys = k_ref[:, :, sl].reshape(ROWS * CTX, HD)
        nk = new[:, 0, sl].astype(BF16)
        s = lax.dot_general(q, keys, nt, preferred_element_type=F32) * scale
        so = lax.dot_general(q, nk, nt, preferred_element_type=F32) * scale
        scores.append(jnp.where(valid, s, -jnp.inf))
        owns.append(jnp.where(own_valid, so, -jnp.inf))
    tops = [
        jnp.maximum(jnp.max(s, axis=1, keepdims=True), jnp.max(so, axis=1, keepdims=True))
        for s, so in zip(scores, owns)
    ]
    es = [jnp.exp(s - t) for s, t in zip(scores, tops)]
    eos = [jnp.exp(so - t) for so, t in zip(owns, tops)]
    totals = [
        jnp.sum(e, axis=1, keepdims=True) + jnp.sum(eo, axis=1, keepdims=True)
        for e, eo in zip(es, eos)
    ]
    for c in copies[4:]:
        c.wait()
    for k in range(LOCAL_HEADS):
        sl = slice(k * HD, (k + 1) * HD)
        vals = v_ref[:, :, sl].reshape(ROWS * CTX, HD)
        nv = new[:, 1, sl].astype(BF16)
        p = (es[k] / totals[k]).astype(BF16)
        po = (eos[k] / totals[k]).astype(BF16)
        attn = jnp.dot(p, vals, preferred_element_type=F32) + jnp.dot(
            po, nv, preferred_element_type=F32
        )
        for g in range(GROUP):
            h = k * GROUP + g
            hs = slice(h * HD, (h + 1) * HD)
            hidden_ref[:, hs] = (
                res_ref[:, hs].astype(F32) + attn[g * ROWS : (g + 1) * ROWS]
            ).astype(BF16)
    for c in range(0, HALF, HD):
        gain_out[:, c : c + HD] = gain_ref[pl.ds(c, HD)].astype(F32).reshape(1, HD)
    ids = [ids_ref[p % 2, p // 2] for p in range(2 * ROWS)]
    rows = slot_rows(ids)
    ri = lax.broadcasted_iota(jnp.int32, (EXPERTS * CAP, ROWS), 0)
    ci = lax.broadcasted_iota(jnp.int32, (EXPERTS * CAP, ROWS), 1)
    select = jnp.zeros((EXPERTS * CAP, ROWS), F32)
    for p in range(2 * ROWS):
        select = jnp.where((ri == rows[p]) & (ci == p // 2), 1.0, select)
    out = jnp.dot(select.astype(BF16), hidden_ref[...], preferred_element_type=F32).astype(BF16)
    for e in range(EXPERTS):
        for a in range(2):
            out_ref[a * EXPERTS + e] = out[e * CAP : (e + 1) * CAP]
    lane = lax.broadcasted_iota(jnp.int32, (ROWS, HD), 1)
    tok = lax.broadcasted_iota(jnp.int32, (ROWS, HD), 0)
    diff = jnp.zeros((ROWS, HD), F32)
    for t in range(ROWS):
        gap = logit_ref[t, ids[2 * t]] - logit_ref[t, ids[2 * t + 1]]
        diff = jnp.where(tok == t, gap, diff)
    wa, wb = jax.nn.sigmoid(diff), jax.nn.sigmoid(-diff)
    place = lane % (EXPERTS * CAP)
    comb = jnp.zeros((ROWS, HD), F32)
    for t in range(ROWS):
        comb = jnp.where((tok == t) & (place == rows[2 * t]), wa, comb)
        comb = jnp.where((tok == t) & (place == rows[2 * t + 1]), wb, comb)
    high = comb.astype(BF16).astype(F32)
    mid = (comb - high).astype(BF16).astype(F32)
    low = comb - high - mid
    comb_ref[...] = jnp.concatenate([high, mid, low, jnp.zeros_like(low)], axis=0).astype(BF16)


def slot_rows(ids):
    rows = []
    for p in range(len(ids)):
        slot = jnp.int32(0)
        for q in range(p):
            slot = slot + (ids[q] == ids[p]).astype(jnp.int32)
        rows.append(ids[p] * CAP + slot)
    return rows


CHUNK = 768
PART = 32


def scale_rows(x_ref, gain_ref, scaled_ref, at, cols, acc):
    for c in range(cols.start, cols.stop, HD):
        part = x_ref[:, c : c + HD].astype(F32)
        acc = acc + part * part
        scaled_ref[at : at + PART, c : c + HD] = (part * gain_ref[:, c : c + HD]).astype(BF16)
    return acc


def put_squares(acc, at, sq_ref, send_ref):
    lane = lax.broadcasted_iota(jnp.int32, (PART, HD), 1)
    total = jnp.broadcast_to(jnp.sum(acc, axis=1, keepdims=True), (PART, HD))
    high = total.astype(BF16).astype(F32)
    low = jnp.where(high < jnp.inf, total - high, 0.0)
    sq_ref[at : at + PART] = total
    send_ref[at : at + PART, 2 * HIDDEN :] = jnp.where(lane < HD // 2, high, low).astype(BF16)


def gate_up(xs, gain_ref, wg_ref, wu_ref, own_ref, sq_ref, send_ref, scaled_ref, chunk):
    accs = [jnp.zeros((PART, HD), F32) for _ in xs]
    sums = [None, None]
    for k in range(0, HALF, chunk):
        rows = slice(k, k + chunk)
        for n, x_ref in enumerate(xs):
            accs[n] = scale_rows(x_ref, gain_ref, scaled_ref, n * PART, rows, accs[n])
        x = scaled_ref[:, rows]
        for i, w_ref in enumerate((wg_ref, wu_ref)):
            got = jnp.dot(x, w_ref[rows], preferred_element_type=F32)
            sums[i] = got if sums[i] is None else sums[i] + got
    for i, at in enumerate((0, HIDDEN)):
        own_ref[:, at : at + HIDDEN] = sums[i]
        send_ref[:, at : at + HIDDEN] = sums[i].astype(BF16)
    for n in range(len(xs)):
        put_squares(accs[n], n * PART, sq_ref, send_ref)


def weight_copies(sources, targets, sems):
    steps = [(k, w) for k in range(0, HALF, CHUNK) for w in (0, 1)]
    copies = []
    for n, (k, w) in enumerate(steps):
        rows = pl.ds(k, CHUNK)
        copies.append(
            pltpu.make_async_copy(sources[w].at[0, rows], targets[w].at[rows], sems.at[n])
        )
    return steps, copies


def ahead_body(after_ref, wg_hbm, wu_hbm, wg_ref, wu_ref, sems):
    del after_ref

    @pl.when(lax.axis_index("role") == 1)
    def _():
        _, copies = weight_copies((wg_hbm, wu_hbm), (wg_ref, wu_ref), sems)
        for c in copies:
            c.start()
        for c in copies:
            c.wait()


def first_body(*refs):
    xs, gain_ref, sources = refs[:5], refs[5], refs[6:8]
    own_ref, sq_ref, send_ref, wg_ref, wu_ref = refs[10:15]
    scaled_ref, sems = refs[15:]
    late = lax.axis_index("role") == 0
    targets = (wg_ref, wu_ref)
    steps, copies = weight_copies(sources, targets, sems)

    @pl.when(late)
    def _():
        for c in copies:
            c.start()

    @pl.when(late)
    def _():
        for n, x_ref in enumerate(xs):
            zero = jnp.zeros((PART, HD), F32)
            acc = scale_rows(x_ref, gain_ref, scaled_ref, n * PART, slice(0, HALF), zero)
            put_squares(acc, n * PART, sq_ref, send_ref)
        for n, (k, w) in enumerate(steps):
            copies[n].wait()
            rows = slice(k, k + CHUNK)
            at = slice(w * HIDDEN, (w + 1) * HIDDEN)
            got = jnp.dot(scaled_ref[:, rows], targets[w][rows], preferred_element_type=F32)
            if k:
                got = got + own_ref[:, at]
            own_ref[:, at] = got
            if k + CHUNK == HALF:
                send_ref[:, at] = got.astype(BF16)
    @pl.when(jnp.logical_not(late))
    def _():
        gate_up(xs, gain_ref, wg_ref, wu_ref, own_ref, sq_ref, send_ref, scaled_ref, 2 * CHUNK)


def second_body(*refs):
    xs, (gain_ref, wg_ref, wu_ref) = refs[:3], refs[3:6]
    own_ref, sq_ref, send_ref, scaled_ref = refs[6:]
    gate_up(xs, gain_ref, wg_ref, wu_ref, own_ref, sq_ref, send_ref, scaled_ref, 2 * CHUNK)


def coordinates():
    role, x, y = (lax.axis_index(n) for n in ("role", "x", "y"))
    first, second = jnp.where(role == 0, y, x), jnp.where(role == 0, x, y)
    return lax.rem(first + 3, 4), lax.rem(second + 3, 4)


def down_body(blocks, splits, own0, sq0, own1, sq1, got0, got1, wd_ref, *rest):
    outs, act_ref = rest[: len(splits)], rest[len(splits)]
    early, late = got0.shape[0], got1.shape[0]
    my_a, my_b = coordinates()
    for n, (jp, jb) in enumerate(blocks):
        for ai in range(2):
            at = (jp * 8 + jb * 2 + ai) * 16
            ours, sqs, mine = (own0, sq0, at) if at < early else (own1, sq1, at - early)
            away = lax.rem(my_a - 2 * lax.rem(my_a // 2 + jp, 2) - ai + 4, 4)
            peer_b = jnp.where(away == 2, 1, jnp.where(away == 1, 2, away))
            peer_a = lax.rem(my_b - SHIFTS[jb] + 4, 4)
            peer_p = lax.rem(peer_a // 2 + my_b // 2, 2)
            peer = (peer_p * 8 + peer_b * 2 + lax.rem(peer_a, 2)) * 16
            first = pl.multiple_of(jnp.minimum(peer, early - 16), 16)
            second = pl.multiple_of(jnp.clip(peer - early, 0, late - 16), 16)
            got = jnp.where(
                peer < early,
                got0[pl.ds(first, 16)].astype(F32),
                got1[pl.ds(second, 16)].astype(F32),
            )
            lane = 2 * HIDDEN
            extra = got[:, lane : lane + 1] + got[:, lane + HD // 2 : lane + HD // 2 + 1]
            total = sqs[mine : mine + 16][:, :1] + extra
            inv = lax.rsqrt(total / MODEL_WIDTH + 1e-05)
            pre = ours[mine : mine + 16] + got[:, : 2 * HIDDEN]
            pre = jnp.where(inv > 0.0, pre * inv, 0.0)
            gate = pre[:, :HIDDEN]
            act = gate * jax.nn.sigmoid(gate) * pre[:, HIDDEN:]
            act_ref[(n * 2 + ai) * 16 : (n * 2 + ai + 1) * 16] = act.astype(BF16)
    act = act_ref[...]
    for c in range(0, HALF, 512):
        got = jnp.dot(act, wd_ref[:, c : c + 512], preferred_element_type=F32).astype(BF16)
        start = 0
        for out_ref, rows in zip(outs, splits):
            out_ref[:, c : c + 512] = got[start : start + rows]
            start += rows


def sum_body(*refs):
    total = refs[0][...].astype(F32)
    for r in refs[1:-1]:
        total = total + r[...].astype(F32)
    refs[-1][...] = total.astype(BF16)


def combine_body(comb_ref, hidden_ref, back_ref, out_ref):
    got = jnp.dot(comb_ref[:, :PART], back_ref[...], preferred_element_type=F32)
    moe = got[:ROWS] + got[ROWS : 2 * ROWS] + got[2 * ROWS : 3 * ROWS]
    out_ref[...] = (hidden_ref[...].astype(F32) + moe).astype(BF16)


def index_of(role, z, x, y):
    return ((role * 8 + z) * 4 + x) * 4 + y


def permutation(move):
    return [
        (index_of(r, z, x, y), index_of(*move(r, z, x, y)))
        for r in range(2)
        for z in range(8)
        for x in range(4)
        for y in range(4)
    ]


def along_x(s, r, z, x, y):
    return r, z, (x + s) % 4, y


def along_y(s, r, z, x, y):
    return r, z, x, (y + s) % 4


def send_b(value, s):
    return lax.ppermute(
        value,
        AXES,
        permutation(lambda r, z, x, y: along_x(s, r, z, x, y) if r == 0 else along_y(s, r, z, x, y)),
    )


def send_a(value):
    return lax.ppermute(
        value,
        AXES,
        permutation(lambda r, z, x, y: (r, z, x, y ^ 1) if r == 0 else (r, z, x ^ 1, y)),
    )


def swap(value):
    return lax.ppermute(value, "role", [(0, 1), (1, 0)])


def exchange(value):
    groups = []
    for p in (1, 3):
        for o in range(4):
            pair = [(a, z) for a in (p, (p + 1) % 4) for z in range(8)]
            groups.append([index_of(0, z, o, a) for a, z in pair])
            groups.append([index_of(1, z, a, o) for a, z in pair])
    return lax.all_to_all(
        value, AXES, split_axis=0, concat_axis=0, axis_index_groups=groups, tiled=True
    )


def per_device(
    query, new_kv, kv_cache, lengths, residual, norm_gain, expert_ids, router_logits, w_gate, w_up, w_down
):
    shape = jax.ShapeDtypeStruct
    hidden, outgoing, comb, gain = call(
        attend_body,
        (shape((ROWS, HALF), BF16), shape((2 * EXPERTS, CAP, HALF), BF16), shape((4 * ROWS, HD), BF16), shape((1, HALF), F32)),
        [HBM_SPEC] * 8,
        flops=50_000_000,
        nbytes=1_200_000,
        scratch=[
            pltpu.SMEM((ROWS,), jnp.int32),
            pltpu.SMEM((2, ROWS), jnp.int32),
            pltpu.SMEM((ROWS, EXPERTS), F32),
            pltpu.VMEM((ROWS, HALF), BF16),
            pltpu.VMEM((ROWS, 2, HIDDEN), BF16),
            pltpu.VMEM((ROWS, CTX, HIDDEN), BF16),
            pltpu.VMEM((ROWS, CTX, HIDDEN), BF16),
            pltpu.VMEM((ROWS, HALF), BF16),
            pltpu.VMEM((HALF,), BF16),
            pltpu.SemaphoreType.DMA((9,)),
        ],
    )(*map(in_hbm, (lengths, expert_ids.T, router_logits, query, new_kv, kv_cache, residual, norm_gain)))
    near = exchange(outgoing).reshape(PART, HALF)
    far = send_a(near)
    blocks = (
        pltpu.VMEM((HALF, HIDDEN), BF16),
        pltpu.VMEM((HALF, HIDDEN), BF16),
    )
    count = 2 * HALF // CHUNK
    sources = tuple(map(in_hbm, (w_gate, w_up)))
    ahead = call(
        ahead_body,
        blocks,
        [VMEM_SPEC] + [HBM_SPEC] * 2,
        nbytes=12_000_000,
        scratch=[pltpu.SemaphoreType.DMA((count,))],
    )(near, *sources)
    near, *ahead = lax.optimization_barrier((near, *ahead))
    near_b = [send_b(near, s) for s in ORDER]
    far_b = [send_b(far, s) for s in ORDER]

    def partials(rows):
        return (
            shape((rows, 2 * HIDDEN), F32),
            shape((rows, HD), F32),
            shape((rows, 2 * HIDDEN + HD), BF16),
        )

    own0, sq0, send0, wg, wu = call(
        first_body,
        partials(5 * PART) + blocks,
        [VMEM_SPEC] * 6 + [HBM_SPEC] * 2 + [VMEM_SPEC] * 2,
        flops=2 * 5 * PART * HALF * 1024,
        nbytes=20_000_000,
        scratch=[
            pltpu.VMEM((5 * PART, HALF), BF16),
            pltpu.SemaphoreType.DMA((count,)),
        ],
        aliases={8: 3, 9: 4},
    )(near, *near_b, far, gain, *sources, *ahead)
    own1, sq1, send1 = call(
        second_body,
        partials(3 * PART),
        [VMEM_SPEC] * 6,
        flops=2 * 3 * PART * HALF * 1024,
        nbytes=8_000_000,
        scratch=[pltpu.VMEM((3 * PART, HALF), BF16)],
    )(*far_b, gain, wg, wu)
    swapped0, swapped1 = swap(send0), swap(send1)

    def down(blocks, splits):
        rows = PART * len(blocks)
        return call(
            functools.partial(down_body, blocks, splits),
            [shape((n, HALF), BF16) for n in splits],
            [VMEM_SPEC] * 7,
            flops=2 * rows * HALF * 512,
            nbytes=5_000_000,
            scratch=[pltpu.VMEM((rows, HIDDEN), BF16)],
        )(own0, sq0, own1, sq1, swapped0, swapped1, w_down[0])

    far_terms = down(tuple((1, j) for j in range(4)), (PART,) * 4)
    near_terms = down(tuple((0, j) for j in range(4)), (PART,) * 4)

    def add_up(*parts):
        return call(
            sum_body,
            shape((PART, HALF), BF16),
            [VMEM_SPEC] * len(parts),
            flops=400_000,
            nbytes=1_000_000,
        )(*parts)

    far_sum = add_up(far_terms[0], *[send_b(far_terms[j], -SHIFTS[j]) for j in (1, 2, 3)])
    near_got = [send_b(near_terms[j], -SHIFTS[j]) for j in (2, 3, 1)]
    summed = add_up(near_terms[0], *near_got, send_a(far_sum))
    back = exchange(summed.reshape(2 * EXPERTS, CAP, HALF)).reshape(PART, HALF)
    return call(
        combine_body,
        shape((ROWS, HALF), BF16),
        [VMEM_SPEC] * 3,
        flops=100_000,
        nbytes=150_000,
    )(comb, hidden, back)


def solution(mesh):
    fine = Mesh(mesh.devices.reshape(2, 8, 4, 4), AXES)
    rows = ("expert", "x", "y")
    shard = ("x", "y")
    in_specs = (
        P(rows, "role"),
        P(rows, None, "role"),
        P(rows, None, None, "role"),
        P(rows),
        P(rows, "role"),
        P("role"),
        P(rows, None),
        P(rows, None),
        P("expert", "role", shard),
        P("expert", "role", shard),
        P("expert", shard, "role"),
    )
    return jax.shard_map(
        per_device, mesh=fine, in_specs=in_specs, out_specs=P(rows, "role"), check_vma=False
    )
```

```python
import functools

import jax
import jax.numpy as jnp
from jax import lax
from jax.experimental import pallas as pl
from jax.experimental.pallas import tpu as pltpu
from jax.sharding import Mesh
from jax.sharding import PartitionSpec as P

MODEL_WIDTH = 6144
HALF = 3072
GROUP = 6
HD = 128
CTX = 128
ROWS = 4
LOCAL_HEADS = 4
EXPERTS = 8
CAP = 2
HIDDEN = 512
AXES = ("role", "expert", "x", "y")
ORDER = (2, 1, -1)
SHIFTS = (0,) + ORDER
VMEM_SPEC = pl.BlockSpec(memory_space=pltpu.VMEM)
HBM_SPEC = pl.BlockSpec(memory_space=pltpu.HBM)
F32 = jnp.float32
BF16 = jnp.bfloat16


def call(body, out_shape, in_specs, flops=0, nbytes=0, scratch=(), aliases=None):
    single = not isinstance(out_shape, (tuple, list))
    out_specs = VMEM_SPEC if single else [VMEM_SPEC] * len(out_shape)
    return pl.pallas_call(
        body,
        out_shape=out_shape,
        in_specs=in_specs,
        out_specs=out_specs,
        scratch_shapes=list(scratch),
        input_output_aliases=aliases or {},
        compiler_params=pltpu.CompilerParams(vmem_limit_bytes=16 * 1024 * 1024),
        cost_estimate=pl.CostEstimate(flops=flops, bytes_accessed=nbytes, transcendentals=0),
    )


def in_hbm(value):
    return pltpu.with_memory_space_constraint(value, pltpu.HBM)


def attend_body(
    len_hbm, ids_hbm, logit_hbm, q_hbm, new_hbm, kv_hbm, res_hbm, gain_hbm,
    hidden_ref, out_ref, comb_ref, gain_out,
    len_ref, ids_ref, logit_ref, q_ref, new_ref, k_ref, v_ref, res_ref, gain_ref, sems,
):
    pairs = (
        (kv_hbm.at[:, 0], k_ref),
        (q_hbm, q_ref),
        (len_hbm, len_ref),
        (new_hbm, new_ref),
        (kv_hbm.at[:, 1], v_ref),
        (res_hbm, res_ref),
        (ids_hbm, ids_ref),
        (logit_hbm, logit_ref),
        (gain_hbm, gain_ref),
    )
    copies = [pltpu.make_async_copy(a, b, sems.at[i]) for i, (a, b) in enumerate(pairs)]
    for c in copies:
        c.start()
    scale = 1.0 / HD**0.5
    m_rows = GROUP * ROWS
    nt = (((1,), (1,)), ((), ()))
    for c in copies[:4]:
        c.wait()
    row_req = lax.broadcasted_iota(jnp.int32, (m_rows, 1), 0) % ROWS
    row_len = jnp.zeros((m_rows, 1), jnp.int32)
    for r in range(ROWS):
        row_len = jnp.where(row_req == r, len_ref[r], row_len)
    col = lax.broadcasted_iota(jnp.int32, (m_rows, ROWS * CTX), 1)
    valid = (col // CTX == row_req) & (col % CTX < row_len)
    own_valid = lax.broadcasted_iota(jnp.int32, (m_rows, ROWS), 1) == row_req
    new = new_ref[...].astype(F32)
    scores, owns = [], []
    for k in range(LOCAL_HEADS):
        sl = slice(k * HD, (k + 1) * HD)
        q = jnp.concatenate(
            [
                q_ref[:, (k * GROUP + g) * HD : (k * GROUP + g + 1) * HD].astype(F32)
                for g in range(GROUP)
            ],
            axis=0,
        ).astype(BF16)
        keys = k_ref[:, :, sl].reshape(ROWS * CTX, HD)
        nk = new[:, 0, sl].astype(BF16)
        s = lax.dot_general(q, keys, nt, preferred_element_type=F32) * scale
        so = lax.dot_general(q, nk, nt, preferred_element_type=F32) * scale
        scores.append(jnp.where(valid, s, -jnp.inf))
        owns.append(jnp.where(own_valid, so, -jnp.inf))
    tops = [
        jnp.maximum(jnp.max(s, axis=1, keepdims=True), jnp.max(so, axis=1, keepdims=True))
        for s, so in zip(scores, owns)
    ]
    es = [jnp.exp(s - t) for s, t in zip(scores, tops)]
    eos = [jnp.exp(so - t) for so, t in zip(owns, tops)]
    totals = [
        jnp.sum(e, axis=1, keepdims=True) + jnp.sum(eo, axis=1, keepdims=True)
        for e, eo in zip(es, eos)
    ]
    for c in copies[4:]:
        c.wait()
    for k in range(LOCAL_HEADS):
        sl = slice(k * HD, (k + 1) * HD)
        vals = v_ref[:, :, sl].reshape(ROWS * CTX, HD)
        nv = new[:, 1, sl].astype(BF16)
        p = (es[k] / totals[k]).astype(BF16)
        po = (eos[k] / totals[k]).astype(BF16)
        attn = jnp.dot(p, vals, preferred_element_type=F32) + jnp.dot(
            po, nv, preferred_element_type=F32
        )
        for g in range(GROUP):
            h = k * GROUP + g
            hs = slice(h * HD, (h + 1) * HD)
            hidden_ref[:, hs] = (
                res_ref[:, hs].astype(F32) + attn[g * ROWS : (g + 1) * ROWS]
            ).astype(BF16)
    for c in range(0, HALF, HD):
        gain_out[:, c : c + HD] = gain_ref[pl.ds(c, HD)].astype(F32).reshape(1, HD)
    ids = [ids_ref[p % 2, p // 2] for p in range(2 * ROWS)]
    rows = slot_rows(ids)
    ri = lax.broadcasted_iota(jnp.int32, (EXPERTS * CAP, ROWS), 0)
    ci = lax.broadcasted_iota(jnp.int32, (EXPERTS * CAP, ROWS), 1)
    select = jnp.zeros((EXPERTS * CAP, ROWS), F32)
    for p in range(2 * ROWS):
        select = jnp.where((ri == rows[p]) & (ci == p // 2), 1.0, select)
    out = jnp.dot(select.astype(BF16), hidden_ref[...], preferred_element_type=F32).astype(BF16)
    for e in range(EXPERTS):
        for a in range(2):
            out_ref[a * EXPERTS + e] = out[e * CAP : (e + 1) * CAP]
    lane = lax.broadcasted_iota(jnp.int32, (ROWS, HD), 1)
    tok = lax.broadcasted_iota(jnp.int32, (ROWS, HD), 0)
    diff = jnp.zeros((ROWS, HD), F32)
    for t in range(ROWS):
        gap = logit_ref[t, ids[2 * t]] - logit_ref[t, ids[2 * t + 1]]
        diff = jnp.where(tok == t, gap, diff)
    wa, wb = jax.nn.sigmoid(diff), jax.nn.sigmoid(-diff)
    place = lane % (EXPERTS * CAP)
    comb = jnp.zeros((ROWS, HD), F32)
    for t in range(ROWS):
        comb = jnp.where((tok == t) & (place == rows[2 * t]), wa, comb)
        comb = jnp.where((tok == t) & (place == rows[2 * t + 1]), wb, comb)
    high = comb.astype(BF16).astype(F32)
    mid = (comb - high).astype(BF16).astype(F32)
    low = comb - high - mid
    comb_ref[...] = jnp.concatenate([high, mid, low, jnp.zeros_like(low)], axis=0).astype(BF16)


def slot_rows(ids):
    rows = []
    for p in range(len(ids)):
        slot = jnp.int32(0)
        for q in range(p):
            slot = slot + (ids[q] == ids[p]).astype(jnp.int32)
        rows.append(ids[p] * CAP + slot)
    return rows


CHUNK = 768
PART = 32


def scale_rows(x_ref, gain_ref, scaled_ref, at, cols, acc):
    for c in range(cols.start, cols.stop, HD):
        part = x_ref[:, c : c + HD].astype(F32)
        acc = acc + part * part
        scaled_ref[at : at + PART, c : c + HD] = (part * gain_ref[:, c : c + HD]).astype(BF16)
    return acc


def put_squares(acc, at, sq_ref, send_ref):
    lane = lax.broadcasted_iota(jnp.int32, (PART, HD), 1)
    total = jnp.broadcast_to(jnp.sum(acc, axis=1, keepdims=True), (PART, HD))
    high = total.astype(BF16).astype(F32)
    low = jnp.where(high < jnp.inf, total - high, 0.0)
    sq_ref[at : at + PART] = total
    send_ref[at : at + PART, 2 * HIDDEN :] = jnp.where(lane < HD // 2, high, low).astype(BF16)


def gate_up(xs, gain_ref, wg_ref, wu_ref, own_ref, sq_ref, send_ref, scaled_ref, chunk):
    accs = [jnp.zeros((PART, HD), F32) for _ in xs]
    sums = [None, None]
    for k in range(0, HALF, chunk):
        rows = slice(k, k + chunk)
        for n, x_ref in enumerate(xs):
            accs[n] = scale_rows(x_ref, gain_ref, scaled_ref, n * PART, rows, accs[n])
        x = scaled_ref[:, rows]
        for i, w_ref in enumerate((wg_ref, wu_ref)):
            got = jnp.dot(x, w_ref[rows], preferred_element_type=F32)
            sums[i] = got if sums[i] is None else sums[i] + got
    for i, at in enumerate((0, HIDDEN)):
        kept = sums[i][: own_ref.shape[0]]
        own_ref[:, at : at + HIDDEN] = kept
        send_ref[:, at : at + HIDDEN] = kept.astype(BF16)
    for n in range(len(xs)):
        put_squares(accs[n], n * PART, sq_ref, send_ref)


def weight_copies(sources, targets, sems):
    steps = [(k, w) for k in range(0, HALF, CHUNK) for w in (0, 1)]
    copies = []
    for n, (k, w) in enumerate(steps):
        rows = pl.ds(k, CHUNK)
        copies.append(
            pltpu.make_async_copy(sources[w].at[0, rows], targets[w].at[rows], sems.at[n])
        )
    return steps, copies


def ahead_body(after_ref, wg_hbm, wu_hbm, wg_ref, wu_ref, sems):
    del after_ref

    @pl.when(lax.axis_index("role") == 1)
    def _():
        _, copies = weight_copies((wg_hbm, wu_hbm), (wg_ref, wu_ref), sems)
        for c in copies:
            c.start()
        for c in copies:
            c.wait()


def first_body(*refs):
    xs, gain_ref, sources = refs[:5], refs[5], refs[6:8]
    own_ref, sq_ref, send_ref, wg_ref, wu_ref = refs[10:15]
    scaled_ref, sems = refs[15:]
    late = lax.axis_index("role") == 0
    targets = (wg_ref, wu_ref)
    steps, copies = weight_copies(sources, targets, sems)

    @pl.when(late)
    def _():
        for c in copies:
            c.start()

    @pl.when(late)
    def _():
        for n, x_ref in enumerate(xs):
            zero = jnp.zeros((PART, HD), F32)
            acc = scale_rows(x_ref, gain_ref, scaled_ref, n * PART, slice(0, HALF), zero)
            put_squares(acc, n * PART, sq_ref, send_ref)
        for n, (k, w) in enumerate(steps):
            copies[n].wait()
            rows = slice(k, k + CHUNK)
            at = slice(w * HIDDEN, (w + 1) * HIDDEN)
            got = jnp.dot(scaled_ref[:, rows], targets[w][rows], preferred_element_type=F32)
            if k:
                got = got + own_ref[:, at]
            own_ref[:, at] = got
            if k + CHUNK == HALF:
                send_ref[:, at] = got.astype(BF16)
    @pl.when(jnp.logical_not(late))
    def _():
        gate_up(xs, gain_ref, wg_ref, wu_ref, own_ref, sq_ref, send_ref, scaled_ref, 2 * CHUNK)


def second_body(*refs):
    xs, (gain_ref, wg_ref, wu_ref) = refs[:3], refs[3:6]
    own_ref, sq_ref, send_ref, scaled_ref = refs[6:]
    scaled_ref[3 * PART :] = jnp.zeros((PART, HALF), BF16)
    gate_up(xs, gain_ref, wg_ref, wu_ref, own_ref, sq_ref, send_ref, scaled_ref, 2 * CHUNK)


def coordinates():
    role, x, y = (lax.axis_index(n) for n in ("role", "x", "y"))
    first, second = jnp.where(role == 0, y, x), jnp.where(role == 0, x, y)
    return lax.rem(first + 3, 4), lax.rem(second + 3, 4)


def down_body(blocks, splits, own0, sq0, own1, sq1, got0, got1, wd_ref, *rest):
    outs, act_ref = rest[: len(splits)], rest[len(splits)]
    early, late = got0.shape[0], got1.shape[0]
    my_a, my_b = coordinates()
    for n, (jp, jb) in enumerate(blocks):
        for ai in range(2):
            at = (jp * 8 + jb * 2 + ai) * 16
            ours, sqs, mine = (own0, sq0, at) if at < early else (own1, sq1, at - early)
            away = lax.rem(my_a - 2 * lax.rem(my_a // 2 + jp, 2) - ai + 4, 4)
            peer_b = jnp.where(away == 2, 1, jnp.where(away == 1, 2, away))
            peer_a = lax.rem(my_b - SHIFTS[jb] + 4, 4)
            peer_p = lax.rem(peer_a // 2 + my_b // 2, 2)
            peer = (peer_p * 8 + peer_b * 2 + lax.rem(peer_a, 2)) * 16
            first = pl.multiple_of(jnp.minimum(peer, early - 16), 16)
            second = pl.multiple_of(jnp.clip(peer - early, 0, late - 16), 16)
            got = jnp.where(
                peer < early,
                got0[pl.ds(first, 16)].astype(F32),
                got1[pl.ds(second, 16)].astype(F32),
            )
            lane = 2 * HIDDEN
            extra = got[:, lane : lane + 1] + got[:, lane + HD // 2 : lane + HD // 2 + 1]
            total = sqs[mine : mine + 16][:, :1] + extra
            inv = lax.rsqrt(total / MODEL_WIDTH + 1e-05)
            pre = ours[mine : mine + 16] + got[:, : 2 * HIDDEN]
            pre = jnp.where(inv > 0.0, pre * inv, 0.0)
            gate = pre[:, :HIDDEN]
            act = gate * jax.nn.sigmoid(gate) * pre[:, HIDDEN:]
            act_ref[(n * 2 + ai) * 16 : (n * 2 + ai + 1) * 16] = act.astype(BF16)
    act = act_ref[...]
    for c in range(0, HALF, 512):
        got = jnp.dot(act, wd_ref[:, c : c + 512], preferred_element_type=F32).astype(BF16)
        start = 0
        for out_ref, rows in zip(outs, splits):
            out_ref[:, c : c + 512] = got[start : start + rows]
            start += rows


def sum_body(*refs):
    total = refs[0][...].astype(F32)
    for r in refs[1:-1]:
        total = total + r[...].astype(F32)
    refs[-1][...] = total.astype(BF16)


def combine_body(comb_ref, hidden_ref, back_ref, out_ref):
    got = jnp.dot(comb_ref[:, :PART], back_ref[...], preferred_element_type=F32)
    moe = got[:ROWS] + got[ROWS : 2 * ROWS] + got[2 * ROWS : 3 * ROWS]
    out_ref[...] = (hidden_ref[...].astype(F32) + moe).astype(BF16)


def index_of(role, z, x, y):
    return ((role * 8 + z) * 4 + x) * 4 + y


def permutation(move):
    return [
        (index_of(r, z, x, y), index_of(*move(r, z, x, y)))
        for r in range(2)
        for z in range(8)
        for x in range(4)
        for y in range(4)
    ]


def along_x(s, r, z, x, y):
    return r, z, (x + s) % 4, y


def along_y(s, r, z, x, y):
    return r, z, x, (y + s) % 4


def send_b(value, s):
    return lax.ppermute(
        value,
        AXES,
        permutation(lambda r, z, x, y: along_x(s, r, z, x, y) if r == 0 else along_y(s, r, z, x, y)),
    )


def send_a(value):
    return lax.ppermute(
        value,
        AXES,
        permutation(lambda r, z, x, y: (r, z, x, y ^ 1) if r == 0 else (r, z, x ^ 1, y)),
    )


def swap(value):
    return lax.ppermute(value, "role", [(0, 1), (1, 0)])


def exchange(value):
    groups = []
    for p in (1, 3):
        for o in range(4):
            pair = [(a, z) for a in (p, (p + 1) % 4) for z in range(8)]
            groups.append([index_of(0, z, o, a) for a, z in pair])
            groups.append([index_of(1, z, a, o) for a, z in pair])
    return lax.all_to_all(
        value, AXES, split_axis=0, concat_axis=0, axis_index_groups=groups, tiled=True
    )


def per_device(
    query, new_kv, kv_cache, lengths, residual, norm_gain, expert_ids, router_logits, w_gate, w_up, w_down
):
    shape = jax.ShapeDtypeStruct
    hidden, outgoing, comb, gain = call(
        attend_body,
        (shape((ROWS, HALF), BF16), shape((2 * EXPERTS, CAP, HALF), BF16), shape((4 * ROWS, HD), BF16), shape((1, HALF), F32)),
        [HBM_SPEC] * 8,
        flops=50_000_000,
        nbytes=1_200_000,
        scratch=[
            pltpu.SMEM((ROWS,), jnp.int32),
            pltpu.SMEM((2, ROWS), jnp.int32),
            pltpu.SMEM((ROWS, EXPERTS), F32),
            pltpu.VMEM((ROWS, HALF), BF16),
            pltpu.VMEM((ROWS, 2, HIDDEN), BF16),
            pltpu.VMEM((ROWS, CTX, HIDDEN), BF16),
            pltpu.VMEM((ROWS, CTX, HIDDEN), BF16),
            pltpu.VMEM((ROWS, HALF), BF16),
            pltpu.VMEM((HALF,), BF16),
            pltpu.SemaphoreType.DMA((9,)),
        ],
    )(*map(in_hbm, (lengths, expert_ids.T, router_logits, query, new_kv, kv_cache, residual, norm_gain)))
    near = exchange(outgoing).reshape(PART, HALF)
    far = send_a(near)
    blocks = (
        pltpu.VMEM((HALF, HIDDEN), BF16),
        pltpu.VMEM((HALF, HIDDEN), BF16),
    )
    count = 2 * HALF // CHUNK
    sources = tuple(map(in_hbm, (w_gate, w_up)))
    ahead = call(
        ahead_body,
        blocks,
        [VMEM_SPEC] + [HBM_SPEC] * 2,
        nbytes=12_000_000,
        scratch=[pltpu.SemaphoreType.DMA((count,))],
    )(near, *sources)
    near, *ahead = lax.optimization_barrier((near, *ahead))
    near_b = [send_b(near, s) for s in ORDER]
    far_b = [send_b(far, s) for s in ORDER]

    def partials(rows):
        return (
            shape((rows, 2 * HIDDEN), F32),
            shape((rows, HD), F32),
            shape((rows, 2 * HIDDEN + HD), BF16),
        )

    own0, sq0, send0, wg, wu = call(
        first_body,
        partials(5 * PART) + blocks,
        [VMEM_SPEC] * 6 + [HBM_SPEC] * 2 + [VMEM_SPEC] * 2,
        flops=2 * 5 * PART * HALF * 1024,
        nbytes=20_000_000,
        scratch=[
            pltpu.VMEM((5 * PART, HALF), BF16),
            pltpu.SemaphoreType.DMA((count,)),
        ],
        aliases={8: 3, 9: 4},
    )(near, *near_b, far, gain, *sources, *ahead)
    own1, sq1, send1 = call(
        second_body,
        partials(3 * PART),
        [VMEM_SPEC] * 6,
        flops=2 * 3 * PART * HALF * 1024,
        nbytes=8_000_000,
        scratch=[pltpu.VMEM((4 * PART, HALF), BF16)],
    )(*far_b, gain, wg, wu)
    swapped0, swapped1 = swap(send0), swap(send1)

    def down(blocks, splits):
        rows = PART * len(blocks)
        return call(
            functools.partial(down_body, blocks, splits),
            [shape((n, HALF), BF16) for n in splits],
            [VMEM_SPEC] * 7,
            flops=2 * rows * HALF * 512,
            nbytes=5_000_000,
            scratch=[pltpu.VMEM((rows, HIDDEN), BF16)],
        )(own0, sq0, own1, sq1, swapped0, swapped1, w_down[0])

    far_terms = down(tuple((1, j) for j in range(4)), (PART,) * 4)
    near_terms = down(tuple((0, j) for j in range(4)), (PART,) * 4)

    def add_up(*parts):
        return call(
            sum_body,
            shape((PART, HALF), BF16),
            [VMEM_SPEC] * len(parts),
            flops=400_000,
            nbytes=1_000_000,
        )(*parts)

    far_sum = add_up(far_terms[0], *[send_b(far_terms[j], -SHIFTS[j]) for j in (1, 2, 3)])
    near_got = [send_b(near_terms[j], -SHIFTS[j]) for j in (2, 3, 1)]
    summed = add_up(near_terms[0], *near_got, send_a(far_sum))
    back = exchange(summed.reshape(2 * EXPERTS, CAP, HALF)).reshape(PART, HALF)
    return call(
        combine_body,
        shape((ROWS, HALF), BF16),
        [VMEM_SPEC] * 3,
        flops=100_000,
        nbytes=150_000,
    )(comb, hidden, back)


def solution(mesh):
    fine = Mesh(mesh.devices.reshape(2, 8, 4, 4), AXES)
    rows = ("expert", "x", "y")
    shard = ("x", "y")
    in_specs = (
        P(rows, "role"),
        P(rows, None, "role"),
        P(rows, None, None, "role"),
        P(rows),
        P(rows, "role"),
        P("role"),
        P(rows, None),
        P(rows, None),
        P("expert", "role", shard),
        P("expert", "role", shard),
        P("expert", shard, "role"),
    )
    return jax.shard_map(
        per_device, mesh=fine, in_specs=in_specs, out_specs=P(rows, "role"), check_vma=False
    )
```
